128 devices in a mesh: section: 4 (over y), dp: 32 (over z, x, core).
Axes of the slice: x: 4, y: 4, z: 4, core: 2. Of those that a mesh axis runs over, the one named last changes fastest.
Arguments:
- features: bfloat16 [2, 32768, 512], P(None, 'dp'), may hold values from -6 to 6
- w_self: bfloat16 [4, 512, 512], P('section'), may hold values from -0.25 to 0.25
- w_neigh: bfloat16 [4, 512, 512], P('section'), may hold values from -0.75 to 0.75
- bias: float32 [4, 512], P('section'), may hold values from -3 to 3
- gain: float32 [4, 512], P('section'), may hold values from 0.5 to 1.5
- hubs: int32 [2, 32, 32], P(None, None, 'dp'), may hold values from -1 to 7, as said below
- tile_src: int32 [2, 256, 6], P(None, 'dp'), may hold values from 0 to 39, as said below
- counts: int32 [2, 256, 6, 128, 128], P(None, 'dp'), may hold values from 0 to 2, as said below
Outputs:
- acts: bfloat16 [4, 2, 32768, 512], P('section', None, 'dp')
The draws below stay inside these ranges and needn't reach their ends.
Inputs may be any that keep to these rules, and one draw needn't show every extreme that they name: hubs[m, r, r] = -1; hubs[m, r, (r + 1) % 32] is never -1; other entries are -1 or a block index of partition q. `tile_src`: a slot 8 + q appears only where hubs[m, p, q] is not -1 for the tile's partition p. `counts`: some vertices have no edges at all.
All inputs are finite; a program needn't handle non-finite values.
Results may differ from the reference program's by a relative error of at most 0.007.
Values may be sent and summed in bfloat16 or wider, within the bound.
No kernel may reach another device: no remote copies, remote signals or barrier semaphores. Data moves between devices by JAX's collectives and lax.ppermute only.
A program may use at most 128 MiB of HBM per device.

```python
import jax
import jax.numpy as jnp
from jax import lax

D = 512
BLOCK = 128
TPB = 6
MICRO = 2
NB = 8
VERTS = 32768
N_SECTION = 4
N_DP = 32


def hub_table(key):
    key = jax.random.fold_in(key, 11)
    key_level, key_roll, key_block = jax.random.split(key, 3)
    level = jax.random.randint(key_level, (MICRO, N_DP, 1), 35, 91)
    roll = jax.random.randint(key_roll, (MICRO, N_DP, N_DP), 0, 100)
    rows = jnp.arange(N_DP)[:, None]
    cols = jnp.arange(N_DP)[None, :]
    is_hub = (roll < level) & (rows != cols)
    is_hub = is_hub | (cols == (rows + 1) % N_DP)
    chosen = jax.random.randint(key_block, (MICRO, N_DP, N_DP), 0, NB)
    return jnp.where(is_hub, chosen, -1).astype(jnp.int32)


def draw_hubs(key, part):
    return hub_table(key)


def draw_tile_src(key, part):
    table = hub_table(key)
    key = jax.random.fold_in(key, 5)
    key_score, key_local, key_kind = jax.random.split(key, 3)
    live_rows = jnp.repeat(table >= 0, NB, axis=1)
    scores = jax.random.randint(key_score, (MICRO, N_DP * NB, TPB, N_DP), 1, 2 ** 20)
    scores = jnp.where(live_rows[:, :, None, :], scores, 0)
    owner = jnp.argmax(scores, axis=-1).astype(jnp.int32)
    local_slot = jax.random.randint(key_local, (MICRO, N_DP * NB, TPB), 0, NB)
    use_hub = jax.random.randint(key_kind, (MICRO, N_DP * NB, TPB), 0, 2) == 1
    return jnp.where(use_hub, NB + owner, local_slot).astype(jnp.int32)


def draw_counts(key, part):
    key = jax.random.fold_in(key, 7)
    key_mult, key_edge, key_row = jax.random.split(key, 3)
    shape = (MICRO, N_DP * NB, TPB, BLOCK, BLOCK)
    multiple = jax.random.randint(key_mult, shape, 1, 3)
    has_edge = jax.random.randint(key_edge, shape, 0, BLOCK) < 4
    row_live = jax.random.randint(key_row, (MICRO, N_DP * NB, 1, BLOCK, 1), 0, 16) != 0
    return jnp.where(has_edge & row_live, multiple, 0).astype(jnp.int32)


def block_levels(stream_key, shape, shards, smallest, largest):
    def one(dim, shards_of):
        draws = jax.random.uniform(jax.random.fold_in(jax.random.fold_in(stream_key, 6), dim), (shards_of,), jnp.float32, smallest / len(shards), largest / len(shards))
        return jnp.repeat(jnp.exp(draws), shape[dim] // shards_of).reshape((-1,) + (1,) * (len(shape) - dim - 1))

    loudness = one(*shards[0])
    for cut in shards[1:]:
        loudness = loudness * one(*cut)
    return loudness


def normal_values(stream_key, extent, width, bound, shards=(), kind=jnp.bfloat16):
    result = jax.random.normal(stream_key, extent, jnp.float32) * width
    if len(shards) > 0:
        result = block_levels(stream_key, extent, shards, -0.22, 0.18) * result
    return jnp.clip(result, min=-bound, max=bound).astype(kind)


def setup_inputs(seed: int = 0) -> dict:
    key_of = jax.random.split(jax.random.key(seed), 9)
    features = normal_values(key_of[0], (MICRO, VERTS, D), 1.0, 6.0, ((1, 32),))
    w_self = normal_values(key_of[1], (N_SECTION, D, D), D ** -0.5, 0.25, ((0, 4),))
    w_neigh = normal_values(key_of[2], (N_SECTION, D, D), (D // 9) ** -0.5, 0.75, ((0, 4),))
    bias = normal_values(key_of[3], (N_SECTION, D), 0.5, 3.0, ((0, 4),), jnp.float32)
    gain = jnp.clip(1.0 + 0.1 * jax.random.normal(key_of[4], (N_SECTION, D), jnp.float32), 0.5, 1.5)
    hubs = draw_hubs(jax.random.fold_in(key_of[8], 71), 0)
    tile_src = draw_tile_src(jax.random.fold_in(key_of[8], 71), 0)
    counts = draw_counts(jax.random.fold_in(key_of[8], 71), 0)
    return {"features": features, "w_self": w_self, "w_neigh": w_neigh, "bias": bias, "gain": gain, "hubs": hubs, "tile_src": tile_src, "counts": counts}


def aggregate_all(h_all, hub_rows, slot_rows, count_rows):
    blocks_all = h_all.reshape(N_DP, NB, BLOCK, D)
    owners = jnp.arange(N_DP, dtype=jnp.int32)

    def one_part(args):
        part_idx, hub_row, tile_slots, tile_counts = args
        own_blocks = lax.dynamic_index_in_dim(blocks_all, part_idx, 0, keepdims=False)
        clipped = jnp.clip(hub_row, 0, NB - 1).astype(jnp.int32)
        far_blocks = blocks_all[owners, clipped]
        far_blocks = jnp.where((hub_row >= 0)[:, None, None], far_blocks, jnp.zeros_like(far_blocks))
        slot_table = jnp.concatenate([own_blocks, far_blocks], axis=0)
        gathered = slot_table[tile_slots].astype(jnp.float32)
        summed = jnp.einsum('bjvu,bjud->bvd', tile_counts.astype(jnp.float32), gathered)
        degree = lax.optimization_barrier(jnp.sum(tile_counts, axis=(1, 3))).astype(jnp.float32)
        return (summed / jnp.maximum(degree, 1.0)[:, :, None]).astype(jnp.bfloat16)
    aggs = lax.map(one_part, (owners, hub_rows, slot_rows.reshape(N_DP, NB, TPB), count_rows.reshape(N_DP, NB, TPB, BLOCK, BLOCK)))
    return aggs.reshape(VERTS, D)

def sage_layer(h_all, hub_rows, slot_rows, count_rows, self_weight, neigh_weight, bias_row, gain_row):
    neighbor_mean = aggregate_all(h_all, hub_rows, slot_rows, count_rows)
    pre_norm = jnp.dot(h_all, self_weight, preferred_element_type=jnp.float32)
    pre_norm = pre_norm + jnp.dot(neighbor_mean, neigh_weight, preferred_element_type=jnp.float32) + bias_row
    row_mean = lax.optimization_barrier(jnp.mean(pre_norm, axis=-1, keepdims=True))
    row_var = lax.optimization_barrier(jnp.mean((pre_norm - row_mean) ** 2, axis=-1, keepdims=True))
    normed = (pre_norm - row_mean) * lax.rsqrt(row_var + 1e-05) * gain_row
    return jnp.maximum(normed, 0.0).astype(jnp.bfloat16)

def reference(features, w_self, w_neigh, bias, gain, hubs, tile_src, counts):
    layers_out = []
    previous = features
    for layer_idx in range(N_SECTION):
        current = []
        for micro_idx in range(MICRO):
            current.append(sage_layer(previous[micro_idx], hubs[micro_idx], tile_src[micro_idx], counts[micro_idx], w_self[layer_idx], w_neigh[layer_idx], bias[layer_idx], gain[layer_idx]))
        previous = jnp.stack(current)
        layers_out.append(previous)
    return jnp.stack(layers_out)
```

```python
import functools

import jax
import jax.numpy as jnp
from jax import lax
from jax.experimental import pallas as pl
from jax.experimental.pallas import tpu as pltpu
from jax.sharding import Mesh, PartitionSpec as P

SECTION = ("sm", "se")
PARTS = ("dk", "dc")
VMEM_BYTES = 40 * 1024 * 1024
HBM = pltpu.HBM


def params():
    return pltpu.CompilerParams(vmem_limit_bytes=VMEM_BYTES)


def start_picks(meta, source, outgoing, sems):
    n_dest = outgoing.shape[0]
    half = n_dest // 2
    for j in range(n_dest):
        reader = 2 * (j % half) + j // half
        block = jnp.maximum(meta[reader], 0)
        pltpu.make_async_copy(source.at[block], outgoing.at[j], sems.at[j]).start()


def wait_picks(source, outgoing, sems):
    for j in range(outgoing.shape[0]):
        pltpu.make_async_copy(source.at[0], outgoing.at[j], sems.at[j]).wait()


def pick_kernel(meta, source, outgoing, sems):
    start_picks(meta, source, outgoing, sems)
    wait_picks(source, outgoing, sems)


def pick(meta, own):
    n_dest = meta.shape[0] - 48
    return pl.pallas_call(
        pick_kernel,
        out_shape=jax.ShapeDtypeStruct((n_dest,) + own.shape[1:], own.dtype),
        in_specs=[
            pl.BlockSpec(memory_space=pltpu.SMEM),
            pl.BlockSpec(memory_space=pltpu.VMEM),
        ],
        out_specs=pl.BlockSpec(memory_space=HBM),
        scratch_shapes=[pltpu.SemaphoreType.DMA((n_dest,))],
        compiler_params=params(),
        name="pick",
    )(meta, own)


def aggregate_kernel(n_hubs, meta, own, received, counts, inverse, out, table, held, table_sems, count_sems):
    n_blocks, tiles = own.shape[0], 6
    own_copy = pltpu.make_async_copy(own, table.at[pl.ds(0, n_blocks)], table_sems.at[0])
    hub_copy = pltpu.make_async_copy(received, table.at[pl.ds(n_blocks, n_hubs)], table_sems.at[1])
    hub_copy.start()
    own_copy.start()
    count_copies = [
        pltpu.make_async_copy(counts.at[b], held.at[b], count_sems.at[b]) for b in range(n_blocks)
    ]
    for copy in count_copies:
        copy.start()
    own_copy.wait()
    hub_copy.wait()
    width = out.shape[-1]
    for b in range(n_blocks):
        count_copies[b].wait()
        picked = []
        for j in range(tiles):
            slot = meta[n_hubs + b * tiles + j]
            owner = slot - n_blocks
            place = jnp.where(
                slot < n_blocks, slot, n_blocks + lax.rem(owner, 2) * (n_hubs // 2) + lax.div(owner, 2)
            )
            picked.append(table[place])
        summed = jnp.dot(held[b], jnp.concatenate(picked, axis=0), preferred_element_type=jnp.float32)
        scale = inverse[b]
        scale = jnp.concatenate([scale] * (width // scale.shape[-1]), axis=-1)
        out[b] = (summed * scale).astype(out.dtype)


def aggregate(meta, own, received, counts, inverse):
    n_hubs = received.shape[0]
    n_blocks, rows, width = own.shape
    return pl.pallas_call(
        functools.partial(aggregate_kernel, n_hubs),
        out_shape=jax.ShapeDtypeStruct(own.shape, own.dtype),
        in_specs=[
            pl.BlockSpec(memory_space=pltpu.SMEM),
            pl.BlockSpec(memory_space=HBM),
            pl.BlockSpec(memory_space=HBM),
            pl.BlockSpec(memory_space=HBM),
            pl.BlockSpec(memory_space=pltpu.VMEM),
        ],
        out_specs=pl.BlockSpec(memory_space=pltpu.VMEM),
        scratch_shapes=[
            pltpu.VMEM((n_blocks + n_hubs, rows, width), own.dtype),
            pltpu.VMEM(counts.shape, counts.dtype),
            pltpu.SemaphoreType.DMA((2,)),
            pltpu.SemaphoreType.DMA((n_blocks,)),
        ],
        compiler_params=params(),
        name="aggregate",
    )(meta, own, received, counts, inverse)


def dense_kernel(last, place, meta, h, mean_mine, mean_other, w_mine, w_other, affine, *rest):
    if last:
        h_out, weights, w_sems = rest
    else:
        h_out, own_out, outgoing, weights, w_sems, pick_sems = rest
    rel, core = place[0], place[1]
    width = h.shape[-1]
    half = width // 2
    mine_cols = pl.ds(core * half, half)
    other_cols = pl.ds((1 - core) * half, half)

    def copies(self_source, neigh_source):
        return [
            pltpu.make_async_copy(self_source.at[rel], weights.at[pl.ds(0, width)], w_sems.at[0]),
            pltpu.make_async_copy(
                neigh_source.at[rel, mine_cols], weights.at[pl.ds(width, half)], w_sems.at[1]
            ),
            pltpu.make_async_copy(
                neigh_source.at[rel, other_cols], weights.at[pl.ds(width + half, half)], w_sems.at[2]
            ),
        ]

    @pl.when(core == 0)
    def _():
        for copy in copies(w_mine, w_other):
            copy.start()

    @pl.when(core != 0)
    def _():
        for copy in copies(w_other, w_mine):
            copy.start()

    for copy in copies(w_mine, w_other):
        copy.wait()
    n_blocks, rows = mean_mine.shape[0], mean_mine.shape[1]
    bias, gain = affine[0:1, :], affine[1:2, :]
    for b in range(n_blocks):
        chunk = pl.ds(b * rows, rows)
        pre = jnp.dot(h[chunk, :], weights[0:width], preferred_element_type=jnp.float32)
        means = jnp.concatenate([mean_mine[b], mean_other[b]], axis=-1)
        pre = pre + jnp.dot(means, weights[width : 2 * width], preferred_element_type=jnp.float32)
        pre = pre + bias
        mu = jnp.mean(pre, axis=-1, keepdims=True)
        centred = pre - mu
        var = jnp.mean(centred * centred, axis=-1, keepdims=True)
        normed = centred * lax.rsqrt(var + 1e-05) * gain
        value = jnp.maximum(normed, 0.0).astype(h_out.dtype)
        h_out[chunk, :] = value
        if not last:
            own_out[b] = jnp.where(core == 0, value[:, :half], value[:, half:])
    if not last:
        start_picks(meta, own_out, outgoing, pick_sems)
        wait_picks(own_out, outgoing, pick_sems)


def dense(last, n_hubs, place, meta, h, mean_mine, mean_other, w_mine, w_other, affine):
    rows, width = h.shape
    vmem, smem, hbm = (pl.BlockSpec(memory_space=s) for s in (pltpu.VMEM, pltpu.SMEM, HBM))
    out_shape = [jax.ShapeDtypeStruct(h.shape, h.dtype)]
    out_specs = [vmem]
    scratch = [pltpu.VMEM((2 * width, width), h.dtype), pltpu.SemaphoreType.DMA((3,))]
    if not last:
        out_shape += [
            jax.ShapeDtypeStruct(mean_mine.shape, h.dtype),
            jax.ShapeDtypeStruct((n_hubs,) + mean_mine.shape[1:], h.dtype),
        ]
        out_specs += [vmem, hbm]
        scratch.append(pltpu.SemaphoreType.DMA((n_hubs,)))
    return pl.pallas_call(
        functools.partial(dense_kernel, last),
        out_shape=out_shape,
        in_specs=[smem, smem, vmem, vmem, vmem, hbm, hbm, vmem],
        out_specs=out_specs,
        scratch_shapes=scratch,
        compiler_params=params(),
        name="dense",
    )(place, meta, h, mean_mine, mean_other, w_mine, w_other, affine)


def swap(value):
    return lax.ppermute(value, "dc", [(0, 1), (1, 0)])


def around(value, by):
    n = lax.axis_size("sm") * lax.axis_size("se")
    return lax.ppermute(value, SECTION, [(i, (i + by) % n) for i in range(n)])


def to_layer(value, layer, graph):
    pairs = [((2 * graph + e) * 2 + e, 2 * layer + e) for e in range(2)]
    return lax.ppermute(value, ("sm", "se", "dc"), pairs)


def body(features, w_self, w_neigh, bias, gain, hubs, tile_src, counts):
    graph, parity = lax.axis_index("sm"), lax.axis_index("se")
    core = lax.axis_index("dc")
    section = 2 * graph + parity
    here = core == parity
    n_layers = 4
    n_blocks, tiles, rows = tile_src.shape[1], tile_src.shape[2], counts.shape[3]
    width = features.shape[2]
    half = width // 2
    n_hubs = hubs.shape[1]

    weight = jnp.where(core == 0, w_self[0], w_neigh[0])
    from_prev, from_next = around(weight, 1), around(weight, -1)

    feats = lax.dynamic_index_in_dim(features, graph, 0, keepdims=False)
    mine = lax.dynamic_slice_in_dim(feats, core * half, half, 1)
    for_other = lax.dynamic_slice_in_dim(feats, (1 - core) * half, half, 1)
    meta = jnp.concatenate(
        [
            lax.dynamic_index_in_dim(hubs, graph, 0, keepdims=False).reshape(-1),
            lax.dynamic_index_in_dim(tile_src, graph, 0, keepdims=False).reshape(-1),
        ]
    )
    meta = jnp.where(here, meta, swap(meta))
    own = jnp.where(here, mine, swap(for_other)).reshape(n_blocks, rows, half)
    outgoing = pick(meta, own)

    opposite = jnp.concatenate(
        [around(from_prev[: width // 2], 1), around(from_next[width // 2 :], -1)], axis=0
    )
    w_mine = jnp.stack([weight, from_next, opposite, from_prev])
    w_other = swap(w_mine)
    affine = jnp.concatenate([bias, gain, jnp.zeros((6, width), jnp.float32)], axis=0)
    affine = lax.all_gather(affine, SECTION)

    other = swap(mine)
    own_flat = own.reshape(-1, half)
    relayed = jnp.where(
        core == 0, jnp.concatenate([own_flat, other], axis=1), jnp.concatenate([other, own_flat], axis=1)
    )
    h = jnp.where(here, feats, relayed)

    tile_counts = lax.dynamic_index_in_dim(counts, graph, 0, keepdims=False).astype(jnp.bfloat16)
    tile_counts = tile_counts.transpose(0, 2, 1, 3).reshape(n_blocks, rows, tiles * rows)
    tile_counts = jnp.where(here, tile_counts, swap(tile_counts))
    degree = jnp.sum(tile_counts.astype(jnp.float32), axis=2, keepdims=True)
    inverse = jnp.broadcast_to(1.0 / jnp.maximum(degree, 1.0), (n_blocks, rows, 128))

    results = None
    for layer in range(n_layers):
        received = lax.all_to_all(outgoing, ("se", "dk"), 0, 0, tiled=True)
        mean_mine = aggregate(meta, own, received, tile_counts, inverse)
        mean_other = swap(mean_mine)
        place = jnp.stack([lax.rem(layer - section + n_layers, n_layers), core]).astype(jnp.int32)
        last = layer == n_layers - 1
        outs = dense(
            last, n_hubs, place, meta, h, mean_mine, mean_other, w_mine, w_other, affine[layer]
        )
        if last:
            (h,) = outs
        else:
            h, own, outgoing = outs
        arrived = jnp.stack([to_layer(h, layer, 0), to_layer(h, layer, 1)])
        results = arrived if results is None else jnp.where(section == layer, arrived, results)
    return results[None]


def solution(mesh):
    n_section, n_dp = mesh.shape["section"], mesh.shape["dp"]
    units = Mesh(mesh.devices.reshape(2, n_section // 2, n_dp // 2, 2), SECTION + PARTS)
    placed = (
        P(None, PARTS, None),
        P(SECTION, None, None),
        P(SECTION, None, None),
        P(SECTION, None),
        P(SECTION, None),
        P(None, None, PARTS),
        P(None, PARTS, None),
        P(None, PARTS, None, None, None),
    )
    return jax.shard_map(
        body, mesh=units, in_specs=placed, out_specs=P(SECTION, None, PARTS, None), check_vma=False
    )
```

```python
import functools

import jax
import jax.numpy as jnp
from jax import lax
from jax.experimental import pallas as pl
from jax.experimental.pallas import tpu as pltpu
from jax.sharding import Mesh, PartitionSpec as P

SECTION = ("sm", "se")
PARTS = ("dz", "dx", "dc")
CHIPS, CORES = ("dx", "se", "dz"), ("dx", "dc", "dz")
SIDE = 4
ROWS = 128
CHUNK = 256
N_LAYERS = 4
SPLIT_ROWS = 16
VMEM, SMEM, HBM = pltpu.VMEM, pltpu.SMEM, pltpu.HBM


MIB = 1024 * 1024


def params(mib=24):
    return pltpu.CompilerParams(vmem_limit_bytes=mib * MIB)


def call(kernel, name, in_spaces, out_shape, out_spaces, scratch=(), mib=24, **kwargs):
    return pl.pallas_call(
        kernel,
        out_shape=out_shape,
        in_specs=[pl.BlockSpec(memory_space=s) for s in in_spaces],
        out_specs=[pl.BlockSpec(memory_space=s) for s in out_spaces],
        scratch_shapes=list(scratch),
        compiler_params=params(mib),
        name=name,
        **kwargs,
    )


def like(array, shape=None):
    return jax.ShapeDtypeStruct(shape or array.shape, array.dtype)


def part(index, size):
    return pl.ds(pl.multiple_of(index * size, size), size)


def block_rows(block):
    return part(block, ROWS)


def run_copies(pieces, sems):
    copies = [pltpu.make_async_copy(s, d, sems.at[i]) for i, (s, d) in enumerate(pieces)]
    for copy in copies:
        copy.start()
    for copy in copies:
        copy.wait()


def reader_of(j):
    x, e, z = j // (2 * SIDE), j // SIDE % 2, j % SIDE
    return 2 * (z * SIDE + x) + e


def place_of(partition):
    chip, e = lax.div(partition, 2), lax.rem(partition, 2)
    z, x = lax.div(chip, SIDE), lax.rem(chip, SIDE)
    return x * (2 * SIDE) + e * SIDE + z


def front_kernel(hubs, features, w_self, w_neigh, bias, gain, outgoing, packed, held, load_sem, w_sem, sems):
    graph, parity, core = lax.axis_index("sm"), lax.axis_index("se"), lax.axis_index("dc")
    width = packed.shape[1]
    load = pltpu.make_async_copy(features.at[graph], held, load_sem)
    load.start()
    for index, source in enumerate((w_self, w_neigh)):

        @pl.when(core == index)
        def _(source=source):
            pltpu.make_async_copy(source.at[0], packed.at[pl.ds(0, width)], w_sem).start()

    values = jnp.concatenate([bias[...], gain[...]], axis=0)
    parts = []
    for _ in range(3):
        part = values.astype(packed.dtype).astype(jnp.float32)
        parts.append(part)
        values = values - part
    parts.append(jnp.zeros((SPLIT_ROWS - 6, width), jnp.float32))
    packed[width : width + SPLIT_ROWS, :] = jnp.concatenate(parts, axis=0).astype(packed.dtype)
    load.wait()
    half = outgoing.shape[2]
    copies = []
    for j in range(outgoing.shape[0]):
        reader = reader_of(j)
        block = jnp.maximum(hubs[graph, reader - reader % 2 + parity], 0)
        source = held.at[block_rows(block), pl.ds((reader % 2) * half, half)]
        copies.append(pltpu.make_async_copy(source, outgoing.at[j], sems.at[j]))
        copies[-1].start()
    pltpu.make_async_copy(w_self.at[0], packed.at[pl.ds(0, width)], w_sem).wait()
    for copy in copies:
        copy.wait()


def front(hubs, features, w_self, w_neigh, bias, gain):
    n_hubs, (_, rows, width) = hubs.shape[1], features.shape
    return call(
        front_kernel,
        "front",
        (SMEM, HBM, HBM, HBM, VMEM, VMEM),
        [like(features, (n_hubs, ROWS, width // 2)), like(w_self, (width + SPLIT_ROWS, width))],
        (HBM, VMEM),
        [
            pltpu.VMEM((rows, width), features.dtype),
            pltpu.SemaphoreType.DMA,
            pltpu.SemaphoreType.DMA,
            pltpu.SemaphoreType.DMA((n_hubs,)),
        ],
        mib=56,
    )(hubs, features, w_self, w_neigh, bias, gain)


def ready_kernel(place, *refs):
    sources, (h, counts, inverse, sems) = refs[:6], refs[6:]
    here = place[1] == place[2]
    for held, want in enumerate((jnp.logical_not(here), here)):

        @pl.when(want)
        def _(held=held):
            feats, tile_counts, inverses = sources[3 * (1 - held) : 3 * (1 - held) + 3]
            feats = feats.at[place[0]]
            run_copies([(feats, h), (tile_counts, counts), (inverses, inverse)], sems)


def ready(place, feats, counts, inverse, feats_swapped, counts_swapped, inverse_swapped):
    _, rows, width = feats.shape
    return call(
        ready_kernel,
        "ready",
        (SMEM,) + (HBM,) * 6,
        [like(feats, (rows, width)), like(counts), like(inverse)],
        (VMEM,) * 3,
        [pltpu.SemaphoreType.DMA((3,))],
    )(place, feats, counts, inverse, feats_swapped, counts_swapped, inverse_swapped)


def tally_kernel(place, counts, out, inverse):
    tiles = counts.shape[2]
    total = jnp.zeros((ROWS, ROWS), jnp.float32)
    for j in range(tiles):
        tile = counts[0, 0, j].astype(jnp.float32)
        total = total + tile
        out[0, :, j * ROWS : (j + 1) * ROWS] = tile.astype(out.dtype)
    degree = jnp.sum(total, axis=1, keepdims=True)
    inverse[0] = jnp.broadcast_to(1.0 / jnp.maximum(degree, 1.0), (ROWS, ROWS))


def tally(place, counts):
    n_blocks, tiles = counts.shape[1], counts.shape[2]
    return pl.pallas_call(
        tally_kernel,
        out_shape=[
            jax.ShapeDtypeStruct((n_blocks, ROWS, tiles * ROWS), jnp.bfloat16),
            jax.ShapeDtypeStruct((n_blocks, ROWS, ROWS), jnp.float32),
        ],
        grid_spec=pltpu.PrefetchScalarGridSpec(
            num_scalar_prefetch=1,
            grid=(n_blocks,),
            in_specs=[pl.BlockSpec((1, 1, tiles, ROWS, ROWS), lambda b, place: (place[0], b, 0, 0, 0))],
            out_specs=[
                pl.BlockSpec((1, ROWS, tiles * ROWS), lambda b, place: (b, 0, 0)),
                pl.BlockSpec((1, ROWS, ROWS), lambda b, place: (b, 0, 0)),
            ],
        ),
        compiler_params=params(),
        name="tally",
    )(place, counts)


def aggregate_kernel(core_ref, tile_src, h, received, counts, inverse, out):
    n_blocks = counts.shape[0]
    tiles = counts.shape[2] // ROWS
    cols = part(core_ref[0], out.shape[1])
    for b in range(n_blocks):
        picked = []
        for j in range(tiles):
            slot = tile_src[b * tiles + j]
            near = h[block_rows(jnp.minimum(slot, n_blocks - 1)), cols]
            sender = place_of(jnp.maximum(slot - n_blocks, 0))
            picked.append(lax.select(slot < n_blocks, near, received[sender]))
        summed = jnp.dot(counts[b], jnp.concatenate(picked, axis=0), preferred_element_type=jnp.float32)
        scale = inverse[b]
        scale = jnp.concatenate([scale] * (out.shape[1] // ROWS), axis=1)
        out[b * ROWS : (b + 1) * ROWS, :] = (summed * scale).astype(out.dtype)


def aggregate(core, tile_src, h, received, counts, inverse):
    rows, width = h.shape
    (out,) = call(
        aggregate_kernel,
        "aggregate",
        (SMEM, SMEM, VMEM, VMEM, VMEM, VMEM),
        [like(h, (rows, width // 2))],
        (VMEM,),
    )(core, tile_src, h, received, counts, inverse)
    return out


def layer_rows(layer, core, rows, h, mean_mine, mean_other, gathered, pre):
    width = h.shape[1]
    half = width // 2
    parts = gathered[2 * layer, width : width + SPLIT_ROWS, :].astype(jnp.float32)
    affine = (parts[4:6] + parts[2:4]) + parts[0:2]
    bias, gain = affine[0:1], affine[1:2]
    left = jnp.concatenate([h[rows, :], mean_mine[rows, :], mean_other[rows, :]], axis=1)
    right = jnp.concatenate(
        [
            gathered[2 * layer, 0:width, :],
            gathered[2 * layer + 1, part(core, half), :],
            gathered[2 * layer + 1, part(1 - core, half), :],
        ],
        axis=0,
    )
    pre[...] = jnp.dot(left, right, preferred_element_type=jnp.float32)
    for begin in range(0, CHUNK, 64):
        x = pre[begin : begin + 64, :] + bias
        mu = jnp.mean(x, axis=1, keepdims=True)
        centred = x - mu
        var = jnp.mean(centred * centred, axis=1, keepdims=True)
        yield begin, jnp.maximum(centred * lax.rsqrt(var + 1e-05) * gain, 0.0).astype(h.dtype)


def dense_kernel(layer, core_ref, blocks, h, mean_mine, mean_other, gathered, h_out, outgoing, pre):
    core = core_ref[0]
    for c in range(h.shape[0] // CHUNK):
        rows = pl.ds(c * CHUNK, CHUNK)
        for begin, value in layer_rows(layer, core, rows, h, mean_mine, mean_other, gathered, pre.at[c]):
            begin = c * CHUNK + begin
            h_out[begin : begin + 64, :] = value
    for j in range(outgoing.shape[0]):
        outgoing[j] = h_out[block_rows(blocks[reader_of(j)]), part(core, outgoing.shape[2])]


def dense(layer, core, blocks, h, mean_mine, mean_other, gathered):
    rows, width = h.shape
    return call(
        functools.partial(dense_kernel, layer),
        "dense",
        (SMEM, SMEM) + (VMEM,) * 4,
        [like(h), like(h, (blocks.shape[0], ROWS, width // 2))],
        (VMEM, VMEM),
        [pltpu.VMEM((rows // CHUNK, CHUNK, width), jnp.float32)],
    )(core, blocks, h, mean_mine, mean_other, gathered)


def last_dense_kernel(core_ref, h, mean_mine, mean_other, gathered, *rest):
    *kept, leaving, pre, sems = rest
    core, last = core_ref[0], N_LAYERS - 1
    half_rows = leaving.shape[1]
    copies = [
        pltpu.make_async_copy(source.at[part(core, half_rows)], leaving.at[layer], sems.at[layer])
        for layer, source in enumerate([*kept, h])
    ]
    for copy in copies:
        copy.start()
    n_chunks = half_rows // CHUNK
    for c in range(n_chunks):
        rows = part(core * n_chunks + c, CHUNK)
        for begin, value in layer_rows(last, core, rows, h, mean_mine, mean_other, gathered, pre.at[c]):
            begin = c * CHUNK + begin
            leaving[last, begin : begin + 64, :] = value
    for copy in copies:
        copy.wait()


def last_dense(core, h, mean_mine, mean_other, gathered, kept):
    rows, width = h.shape
    (out,) = call(
        last_dense_kernel,
        "last_dense",
        (SMEM,) + (VMEM,) * 4 + (HBM,) * len(kept),
        [like(h, (N_LAYERS, rows // 2, width))],
        (VMEM,),
        [
            pltpu.VMEM((rows // 2 // CHUNK, CHUNK, width), jnp.float32),
            pltpu.SemaphoreType.DMA((N_LAYERS - 1,)),
        ],
    )(core, h, mean_mine, mean_other, gathered, *kept)
    return out


def finish_kernel(core_ref, straight, crossed, out, sems):
    core, chunk = core_ref[0], straight.shape[1]
    pieces = []
    for g in range(2):
        pieces.append((straight.at[2 * g + core], out.at[g, part(core, chunk)]))
        pieces.append((crossed.at[g], out.at[g, part(1 - core, chunk)]))
    run_copies(pieces, sems)


def finish(core, straight, crossed):
    _, chunk, width = straight.shape
    (out,) = call(
        finish_kernel,
        "finish",
        (SMEM, VMEM, VMEM),
        [like(straight, (2, 2 * chunk, width))],
        (HBM,),
        [pltpu.SemaphoreType.DMA((4,))],
    )(core, straight, crossed)
    return out


def swap(value):
    return lax.ppermute(value, "dc", [(0, 1), (1, 0)])


def scalars(*values):
    return jnp.stack([jnp.asarray(v).astype(jnp.int32) for v in values])


def body(features, w_self, w_neigh, bias, gain, hubs, tile_src, counts):
    graph, parity = lax.axis_index("sm"), lax.axis_index("se")
    core = lax.axis_index("dc")
    section = 2 * graph + parity
    here = core == parity
    n_hubs = hubs.shape[1]
    place = scalars(graph, parity, core)

    outgoing, packed = front(hubs[:, :, 0], features, w_self, w_neigh, bias, gain)
    gathered = lax.all_gather(packed, SECTION + ("dc",))
    received = lax.all_to_all(outgoing, CORES, 0, 0, tiled=True)

    blocks = jnp.maximum(lax.dynamic_index_in_dim(hubs, graph, 0, keepdims=False).reshape(-1), 0)
    lists = jnp.concatenate(
        [blocks, lax.dynamic_index_in_dim(tile_src, graph, 0, keepdims=False).reshape(-1)]
    )
    lists = jnp.where(here, lists, swap(lists))
    blocks, tiles = lists[:n_hubs], lists[n_hubs:]
    counts, outgoing = lax.optimization_barrier((counts, outgoing))
    tile_counts, inverse = tally(place, counts)
    h, tile_counts, inverse = ready(
        place, features, tile_counts, inverse, swap(features), swap(tile_counts), swap(inverse)
    )
    core_ref, kept = scalars(core), []
    for layer in range(N_LAYERS):
        if layer > 0:
            received = lax.all_to_all(outgoing, CHIPS, 0, 0, tiled=True)
        else:
            received, gathered = lax.optimization_barrier((received, gathered))
        mean_mine = aggregate(core_ref, tiles, h, received, tile_counts, inverse)
        mean_other = swap(mean_mine)
        if layer < N_LAYERS - 1:
            h, outgoing = dense(layer, core_ref, blocks, h, mean_mine, mean_other, gathered)
            kept.append(h)
        else:
            leaving = last_dense(core_ref, h, mean_mine, mean_other, gathered, kept[:-1])
    straight = lax.all_to_all(leaving, SECTION, 0, 0, tiled=True)
    theirs = [lax.dynamic_index_in_dim(straight, 2 * g + 1 - core, 0, keepdims=False) for g in range(2)]
    results = finish(core_ref, straight, swap(jnp.stack(theirs)))
    return results[None]


def solution(mesh):
    n_section, n_dp = mesh.shape["section"], mesh.shape["dp"]
    units = Mesh(mesh.devices.reshape(2, n_section // 2, n_dp // 2 // SIDE, SIDE, 2), SECTION + PARTS)
    placed = (
        P(None, PARTS, None),
        P(SECTION, None, None),
        P(SECTION, None, None),
        P(SECTION, None),
        P(SECTION, None),
        P(None, None, PARTS),
        P(None, PARTS, None),
        P(None, PARTS, None, None, None),
    )
    return jax.shard_map(
        body, mesh=units, in_specs=placed, out_specs=P(SECTION, None, PARTS, None), check_vma=False
    )
```

```python
import functools

import jax
import jax.numpy as jnp
from jax import lax
from jax.experimental import pallas as pl
from jax.experimental.pallas import tpu as pltpu
from jax.sharding import Mesh, PartitionSpec as P

SECTION = ("sm", "se")
PARTS = ("dz", "dx", "dc")
CHIPS, CORES = ("dx", "se", "dz"), ("dx", "dc", "dz")
SIDE = 4
ROWS = 128
CHUNK = 256
N_LAYERS = 4
SPLIT_ROWS = 16
VMEM, SMEM, HBM = pltpu.VMEM, pltpu.SMEM, pltpu.HBM


MIB = 1024 * 1024


def params(mib=24):
    return pltpu.CompilerParams(vmem_limit_bytes=mib * MIB)


def call(kernel, name, in_spaces, out_shape, out_spaces, scratch=(), mib=24, **kwargs):
    return pl.pallas_call(
        kernel,
        out_shape=out_shape,
        in_specs=[pl.BlockSpec(memory_space=s) for s in in_spaces],
        out_specs=[pl.BlockSpec(memory_space=s) for s in out_spaces],
        scratch_shapes=list(scratch),
        compiler_params=params(mib),
        name=name,
        **kwargs,
    )


def like(array, shape=None):
    return jax.ShapeDtypeStruct(shape or array.shape, array.dtype)


def part(index, size):
    return pl.ds(pl.multiple_of(index * size, size), size)


def block_rows(block):
    return part(block, ROWS)


def run_copies(pieces, sems):
    copies = [pltpu.make_async_copy(s, d, sems.at[i]) for i, (s, d) in enumerate(pieces)]
    for copy in copies:
        copy.start()
    for copy in copies:
        copy.wait()


def reader_of(j):
    x, e, z = j // (2 * SIDE), j // SIDE % 2, j % SIDE
    return 2 * (z * SIDE + x) + e


def place_of(partition):
    chip, e = lax.div(partition, 2), lax.rem(partition, 2)
    z, x = lax.div(chip, SIDE), lax.rem(chip, SIDE)
    return x * (2 * SIDE) + e * SIDE + z


def front_kernel(hubs, features, w_self, w_neigh, bias, gain, outgoing, packed, held, load_sem, w_sem, sems):
    graph, parity, core = lax.axis_index("sm"), lax.axis_index("se"), lax.axis_index("dc")
    width = packed.shape[1]
    load = pltpu.make_async_copy(features.at[graph], held, load_sem)
    load.start()
    for index, source in enumerate((w_self, w_neigh)):

        @pl.when(core == index)
        def _(source=source):
            pltpu.make_async_copy(source.at[0], packed.at[pl.ds(0, width)], w_sem).start()

    values = jnp.concatenate([bias[...], gain[...]], axis=0)
    parts = []
    for _ in range(3):
        part = values.astype(packed.dtype).astype(jnp.float32)
        parts.append(part)
        values = values - part
    parts.append(jnp.zeros((SPLIT_ROWS - 6, width), jnp.float32))
    packed[width : width + SPLIT_ROWS, :] = jnp.concatenate(parts, axis=0).astype(packed.dtype)
    load.wait()
    half = outgoing.shape[2]
    copies = []
    for j in range(outgoing.shape[0]):
        reader = reader_of(j)
        block = jnp.maximum(hubs[graph, reader - reader % 2 + parity], 0)
        source = held.at[block_rows(block), pl.ds((reader % 2) * half, half)]
        copies.append(pltpu.make_async_copy(source, outgoing.at[j], sems.at[j]))
        copies[-1].start()
    pltpu.make_async_copy(w_self.at[0], packed.at[pl.ds(0, width)], w_sem).wait()
    for copy in copies:
        copy.wait()


def front(hubs, features, w_self, w_neigh, bias, gain):
    n_hubs, (_, rows, width) = hubs.shape[1], features.shape
    return call(
        front_kernel,
        "front",
        (SMEM, HBM, HBM, HBM, VMEM, VMEM),
        [like(features, (n_hubs, ROWS, width // 2)), like(w_self, (width + SPLIT_ROWS, width))],
        (HBM, VMEM),
        [
            pltpu.VMEM((rows, width), features.dtype),
            pltpu.SemaphoreType.DMA,
            pltpu.SemaphoreType.DMA,
            pltpu.SemaphoreType.DMA((n_hubs,)),
        ],
        mib=56,
    )(hubs, features, w_self, w_neigh, bias, gain)


def ready_kernel(place, *refs):
    sources, (h, counts, inverse, sems) = refs[:6], refs[6:]
    here = place[1] == place[2]
    for held, want in enumerate((jnp.logical_not(here), here)):

        @pl.when(want)
        def _(held=held):
            feats, tile_counts, inverses = sources[3 * (1 - held) : 3 * (1 - held) + 3]
            feats = feats.at[place[0]]
            run_copies([(feats, h), (tile_counts, counts), (inverses, inverse)], sems)


def ready(place, feats, counts, inverse, feats_swapped, counts_swapped, inverse_swapped):
    _, rows, width = feats.shape
    return call(
        ready_kernel,
        "ready",
        (SMEM,) + (HBM,) * 6,
        [like(feats, (rows, width)), like(counts), like(inverse)],
        (VMEM,) * 3,
        [pltpu.SemaphoreType.DMA((3,))],
    )(place, feats, counts, inverse, feats_swapped, counts_swapped, inverse_swapped)


def tally_kernel(place, counts, out, inverse):
    tiles = counts.shape[2]
    total = jnp.zeros((ROWS, ROWS), jnp.float32)
    for j in range(tiles):
        tile = counts[0, 0, j].astype(jnp.float32)
        total = total + tile
        out[0, :, j * ROWS : (j + 1) * ROWS] = tile.astype(out.dtype)
    degree = jnp.sum(total, axis=1, keepdims=True)
    inverse[0] = jnp.broadcast_to(1.0 / jnp.maximum(degree, 1.0), (ROWS, ROWS))


def tally(place, counts):
    n_blocks, tiles = counts.shape[1], counts.shape[2]
    return pl.pallas_call(
        tally_kernel,
        out_shape=[
            jax.ShapeDtypeStruct((n_blocks, ROWS, tiles * ROWS), jnp.bfloat16),
            jax.ShapeDtypeStruct((n_blocks, ROWS, ROWS), jnp.float32),
        ],
        grid_spec=pltpu.PrefetchScalarGridSpec(
            num_scalar_prefetch=1,
            grid=(n_blocks,),
            in_specs=[pl.BlockSpec((1, 1, tiles, ROWS, ROWS), lambda b, place: (place[0], b, 0, 0, 0))],
            out_specs=[
                pl.BlockSpec((1, ROWS, tiles * ROWS), lambda b, place: (b, 0, 0)),
                pl.BlockSpec((1, ROWS, ROWS), lambda b, place: (b, 0, 0)),
            ],
        ),
        compiler_params=params(),
        name="tally",
    )(place, counts)


def aggregate_kernel(core_ref, tile_src, h, received, counts, inverse, out):
    n_blocks = counts.shape[0]
    tiles = counts.shape[2] // ROWS
    cols = part(core_ref[0], out.shape[1])
    for b in range(n_blocks):
        picked = []
        for j in range(tiles):
            slot = tile_src[b * tiles + j]
            near = h[block_rows(jnp.minimum(slot, n_blocks - 1)), cols]
            sender = place_of(jnp.maximum(slot - n_blocks, 0))
            picked.append(lax.select(slot < n_blocks, near, received[sender]))
        summed = jnp.dot(counts[b], jnp.concatenate(picked, axis=0), preferred_element_type=jnp.float32)
        scale = inverse[b]
        scale = jnp.concatenate([scale] * (out.shape[1] // ROWS), axis=1)
        out[b * ROWS : (b + 1) * ROWS, :] = (summed * scale).astype(out.dtype)


def aggregate(core, tile_src, h, received, counts, inverse):
    rows, width = h.shape
    (out,) = call(
        aggregate_kernel,
        "aggregate",
        (SMEM, SMEM, VMEM, VMEM, VMEM, VMEM),
        [like(h, (rows, width // 2))],
        (VMEM,),
    )(core, tile_src, h, received, counts, inverse)
    return out


def layer_rows(layer, core, rows, h, mean_mine, mean_other, gathered, pre):
    width = h.shape[1]
    half = width // 2
    parts = gathered[2 * layer, width : width + SPLIT_ROWS, :].astype(jnp.float32)
    affine = (parts[4:6] + parts[2:4]) + parts[0:2]
    bias, gain = affine[0:1], affine[1:2]
    left = jnp.concatenate([h[rows, :], mean_mine[rows, :], mean_other[rows, :]], axis=1)
    right = jnp.concatenate(
        [
            gathered[2 * layer, 0:width, :],
            gathered[2 * layer + 1, part(core, half), :],
            gathered[2 * layer + 1, part(1 - core, half), :],
        ],
        axis=0,
    )
    pre[...] = jnp.dot(left, right, preferred_element_type=jnp.float32)
    for begin in range(0, CHUNK, 64):
        x = pre[begin : begin + 64, :] + bias
        mu = jnp.mean(x, axis=1, keepdims=True)
        centred = x - mu
        var = jnp.mean(centred * centred, axis=1, keepdims=True)
        yield begin, jnp.maximum(centred * lax.rsqrt(var + 1e-05) * gain, 0.0).astype(h.dtype)


def dense_kernel(layer, core_ref, blocks, h, mean_mine, mean_other, gathered, h_out, outgoing, pre):
    core = core_ref[0]
    for c in range(h.shape[0] // CHUNK):
        rows = pl.ds(c * CHUNK, CHUNK)
        for begin, value in layer_rows(layer, core, rows, h, mean_mine, mean_other, gathered, pre.at[c]):
            begin = c * CHUNK + begin
            h_out[begin : begin + 64, :] = value
    for j in range(outgoing.shape[0]):
        outgoing[j] = h_out[block_rows(blocks[reader_of(j)]), part(core, outgoing.shape[2])]


def dense(layer, core, blocks, h, mean_mine, mean_other, gathered):
    rows, width = h.shape
    return call(
        functools.partial(dense_kernel, layer),
        "dense",
        (SMEM, SMEM) + (VMEM,) * 4,
        [like(h), like(h, (blocks.shape[0], ROWS, width // 2))],
        (VMEM, VMEM),
        [pltpu.VMEM((rows // CHUNK, CHUNK, width), jnp.float32)],
    )(core, blocks, h, mean_mine, mean_other, gathered)


def last_dense_kernel(core_ref, h, mean_mine, mean_other, gathered, *rest):
    *kept, leaving, pre, sems = rest
    core, last = core_ref[0], N_LAYERS - 1
    half_rows = leaving.shape[1]
    copies = [
        pltpu.make_async_copy(source.at[part(core, half_rows)], leaving.at[layer], sems.at[layer])
        for layer, source in enumerate([*kept, h])
    ]
    for copy in copies:
        copy.start()
    n_chunks = half_rows // CHUNK
    for c in range(n_chunks):
        rows = part(core * n_chunks + c, CHUNK)
        for begin, value in layer_rows(last, core, rows, h, mean_mine, mean_other, gathered, pre.at[c]):
            begin = c * CHUNK + begin
            leaving[last, begin : begin + 64, :] = value
    for copy in copies:
        copy.wait()


def last_dense(core, h, mean_mine, mean_other, gathered, kept):
    rows, width = h.shape
    (out,) = call(
        last_dense_kernel,
        "last_dense",
        (SMEM,) + (VMEM,) * 4 + (HBM,) * len(kept),
        [like(h, (N_LAYERS, rows // 2, width))],
        (VMEM,),
        [
            pltpu.VMEM((rows // 2 // CHUNK, CHUNK, width), jnp.float32),
            pltpu.SemaphoreType.DMA((N_LAYERS - 1,)),
        ],
    )(core, h, mean_mine, mean_other, gathered, *kept)
    return out


def finish_kernel(core_ref, straight, crossed, out, sems):
    core, chunk = core_ref[0], straight.shape[1]
    pieces = []
    for g in range(2):
        pieces.append((straight.at[2 * g + core], out.at[g, part(core, chunk)]))
        pieces.append((crossed.at[g], out.at[g, part(1 - core, chunk)]))
    run_copies(pieces, sems)


def finish(core, straight, crossed):
    _, chunk, width = straight.shape
    (out,) = call(
        finish_kernel,
        "finish",
        (SMEM, VMEM, VMEM),
        [like(straight, (2, 2 * chunk, width))],
        (HBM,),
        [pltpu.SemaphoreType.DMA((4,))],
    )(core, straight, crossed)
    return out


def theirs_kernel(core_ref, straight, out, sems):
    core = core_ref[0]
    run_copies([(straight.at[2 * g + 1 - core], out.at[g]) for g in range(2)], sems)


def theirs(core, straight):
    (out,) = call(
        theirs_kernel,
        "theirs",
        (SMEM, VMEM),
        [like(straight, (2,) + straight.shape[1:])],
        (VMEM,),
        [pltpu.SemaphoreType.DMA((2,))],
    )(core, straight)
    return out


def swap(value):
    return lax.ppermute(value, "dc", [(0, 1), (1, 0)])


def scalars(*values):
    return jnp.stack([jnp.asarray(v).astype(jnp.int32) for v in values])


def body(features, w_self, w_neigh, bias, gain, hubs, tile_src, counts):
    graph, parity = lax.axis_index("sm"), lax.axis_index("se")
    core = lax.axis_index("dc")
    section = 2 * graph + parity
    here = core == parity
    n_hubs = hubs.shape[1]
    place = scalars(graph, parity, core)

    outgoing, packed = front(hubs[:, :, 0], features, w_self, w_neigh, bias, gain)
    gathered = lax.all_gather(packed, SECTION + ("dc",))
    received = lax.all_to_all(outgoing, CORES, 0, 0, tiled=True)

    blocks = jnp.maximum(lax.dynamic_index_in_dim(hubs, graph, 0, keepdims=False).reshape(-1), 0)
    lists = jnp.concatenate(
        [blocks, lax.dynamic_index_in_dim(tile_src, graph, 0, keepdims=False).reshape(-1)]
    )
    lists = jnp.where(here, lists, swap(lists))
    blocks, tiles = lists[:n_hubs], lists[n_hubs:]
    counts, outgoing = lax.optimization_barrier((counts, outgoing))
    tile_counts, inverse = tally(place, counts)
    h, tile_counts, inverse = ready(
        place, features, tile_counts, inverse, swap(features), swap(tile_counts), swap(inverse)
    )
    core_ref, kept = scalars(core), []
    for layer in range(N_LAYERS):
        if layer > 0:
            received = lax.all_to_all(outgoing, CHIPS, 0, 0, tiled=True)
        else:
            received, gathered = lax.optimization_barrier((received, gathered))
        mean_mine = aggregate(core_ref, tiles, h, received, tile_counts, inverse)
        mean_other = swap(mean_mine)
        if layer < N_LAYERS - 1:
            h, outgoing = dense(layer, core_ref, blocks, h, mean_mine, mean_other, gathered)
            kept.append(h)
        else:
            leaving = last_dense(core_ref, h, mean_mine, mean_other, gathered, kept[:-1])
    straight = lax.all_to_all(leaving, SECTION, 0, 0, tiled=True)
    results = finish(core_ref, straight, swap(theirs(core_ref, straight)))
    return results[None]


def solution(mesh):
    n_section, n_dp = mesh.shape["section"], mesh.shape["dp"]
    units = Mesh(mesh.devices.reshape(2, n_section // 2, n_dp // 2 // SIDE, SIDE, 2), SECTION + PARTS)
    placed = (
        P(None, PARTS, None),
        P(SECTION, None, None),
        P(SECTION, None, None),
        P(SECTION, None),
        P(SECTION, None),
        P(None, None, PARTS),
        P(None, PARTS, None),
        P(None, PARTS, None, None, None),
    )
    return jax.shard_map(
        body, mesh=units, in_specs=placed, out_specs=P(SECTION, None, PARTS, None), check_vma=False
    )
```

```python
import functools

import jax
import jax.numpy as jnp
from jax import lax
from jax.experimental import pallas as pl
from jax.experimental.pallas import tpu as pltpu
from jax.sharding import Mesh, PartitionSpec as P

SECTION = ("sm", "se")
PARTS = ("dz", "dx", "dc")
CHIPS, CORES = ("dx", "se", "dz"), ("dx", "dc", "dz")
SIDE = 4
ROWS = 128
CHUNK = 256
N_LAYERS = 4
SPLIT_ROWS = 16
VMEM, SMEM, HBM = pltpu.VMEM, pltpu.SMEM, pltpu.HBM


MIB = 1024 * 1024


def params(mib=24):
    return pltpu.CompilerParams(vmem_limit_bytes=mib * MIB)


def call(kernel, name, in_spaces, out_shape, out_spaces, scratch=(), mib=24, **kwargs):
    return pl.pallas_call(
        kernel,
        out_shape=out_shape,
        in_specs=[pl.BlockSpec(memory_space=s) for s in in_spaces],
        out_specs=[pl.BlockSpec(memory_space=s) for s in out_spaces],
        scratch_shapes=list(scratch),
        compiler_params=params(mib),
        name=name,
        **kwargs,
    )


def like(array, shape=None):
    return jax.ShapeDtypeStruct(shape or array.shape, array.dtype)


def part(index, size):
    return pl.ds(pl.multiple_of(index * size, size), size)


def block_rows(block):
    return part(block, ROWS)


def run_copies(pieces, sems):
    copies = [pltpu.make_async_copy(s, d, sems.at[i]) for i, (s, d) in enumerate(pieces)]
    for copy in copies:
        copy.start()
    for copy in copies:
        copy.wait()


def reader_of(j):
    x, e, z = j // (2 * SIDE), j // SIDE % 2, j % SIDE
    return 2 * (z * SIDE + x) + e


def place_of(partition):
    chip, e = lax.div(partition, 2), lax.rem(partition, 2)
    z, x = lax.div(chip, SIDE), lax.rem(chip, SIDE)
    return x * (2 * SIDE) + e * SIDE + z


def front_kernel(hubs, features, w_self, w_neigh, bias, gain, outgoing, packed, held, load_sem, w_sem, sems):
    graph, parity, core = lax.axis_index("sm"), lax.axis_index("se"), lax.axis_index("dc")
    width = packed.shape[1]
    load = pltpu.make_async_copy(features.at[graph], held, load_sem)
    load.start()
    for index, source in enumerate((w_self, w_neigh)):

        @pl.when(core == index)
        def _(source=source):
            pltpu.make_async_copy(source.at[0], packed.at[pl.ds(0, width)], w_sem).start()

    values = jnp.concatenate([bias[...], gain[...]], axis=0)
    parts = []
    for _ in range(3):
        part = values.astype(packed.dtype).astype(jnp.float32)
        parts.append(part)
        values = values - part
    parts.append(jnp.zeros((SPLIT_ROWS - 6, width), jnp.float32))
    packed[width : width + SPLIT_ROWS, :] = jnp.concatenate(parts, axis=0).astype(packed.dtype)
    load.wait()
    half = outgoing.shape[2]
    copies = []
    for j in range(outgoing.shape[0]):
        reader = reader_of(j)
        block = jnp.maximum(hubs[graph, reader - reader % 2 + parity], 0)
        source = held.at[block_rows(block), pl.ds((reader % 2) * half, half)]
        copies.append(pltpu.make_async_copy(source, outgoing.at[j], sems.at[j]))
        copies[-1].start()
    pltpu.make_async_copy(w_self.at[0], packed.at[pl.ds(0, width)], w_sem).wait()
    for copy in copies:
        copy.wait()


def front(hubs, features, w_self, w_neigh, bias, gain):
    n_hubs, (_, rows, width) = hubs.shape[1], features.shape
    return call(
        front_kernel,
        "front",
        (SMEM, HBM, HBM, HBM, VMEM, VMEM),
        [like(features, (n_hubs, ROWS, width // 2)), like(w_self, (width + SPLIT_ROWS, width))],
        (HBM, VMEM),
        [
            pltpu.VMEM((rows, width), features.dtype),
            pltpu.SemaphoreType.DMA,
            pltpu.SemaphoreType.DMA,
            pltpu.SemaphoreType.DMA((n_hubs,)),
        ],
        mib=56,
    )(hubs, features, w_self, w_neigh, bias, gain)


def ready_kernel(place, *refs):
    sources, (h, counts, inverse, sems) = refs[:6], refs[6:]
    here = place[1] == place[2]
    for held, want in enumerate((jnp.logical_not(here), here)):

        @pl.when(want)
        def _(held=held):
            feats, tile_counts, inverses = sources[3 * (1 - held) : 3 * (1 - held) + 3]
            feats = feats.at[place[0]]
            run_copies([(feats, h), (tile_counts, counts), (inverses, inverse)], sems)


def ready(place, feats, counts, inverse, feats_swapped, counts_swapped, inverse_swapped):
    _, rows, width = feats.shape
    return call(
        ready_kernel,
        "ready",
        (SMEM,) + (HBM,) * 6,
        [like(feats, (rows, width)), like(counts), like(inverse)],
        (VMEM,) * 3,
        [pltpu.SemaphoreType.DMA((3,))],
    )(place, feats, counts, inverse, feats_swapped, counts_swapped, inverse_swapped)


def tally_kernel(place, counts, out, inverse):
    tiles = counts.shape[2]
    total = jnp.zeros((ROWS, ROWS), jnp.float32)
    for j in range(tiles):
        tile = counts[0, 0, j].astype(jnp.float32)
        total = total + tile
        out[0, :, j * ROWS : (j + 1) * ROWS] = tile.astype(out.dtype)
    degree = jnp.sum(total, axis=1, keepdims=True)
    inverse[0] = jnp.broadcast_to(1.0 / jnp.maximum(degree, 1.0), (ROWS, ROWS))


def tally(place, counts):
    n_blocks, tiles = counts.shape[1], counts.shape[2]
    return pl.pallas_call(
        tally_kernel,
        out_shape=[
            jax.ShapeDtypeStruct((n_blocks, ROWS, tiles * ROWS), jnp.bfloat16),
            jax.ShapeDtypeStruct((n_blocks, ROWS, ROWS), jnp.float32),
        ],
        grid_spec=pltpu.PrefetchScalarGridSpec(
            num_scalar_prefetch=1,
            grid=(n_blocks,),
            in_specs=[pl.BlockSpec((1, 1, tiles, ROWS, ROWS), lambda b, place: (place[0], b, 0, 0, 0))],
            out_specs=[
                pl.BlockSpec((1, ROWS, tiles * ROWS), lambda b, place: (b, 0, 0)),
                pl.BlockSpec((1, ROWS, ROWS), lambda b, place: (b, 0, 0)),
            ],
        ),
        compiler_params=params(),
        name="tally",
    )(place, counts)


def aggregate_kernel(last, core_ref, tile_src, h, received, counts, inverse, *outs):
    n_blocks = counts.shape[0]
    tiles = counts.shape[2] // ROWS
    core, width = core_ref[0], outs[0].shape[1]
    cols = part(core, width)
    for i in range(n_blocks):
        b = lax.rem(n_blocks // 2 * (1 - core) + i, n_blocks) if last else i
        picked = []
        for j in range(tiles):
            slot = tile_src[b * tiles + j]
            near = h[block_rows(jnp.minimum(slot, n_blocks - 1)), cols]
            sender = place_of(jnp.maximum(slot - n_blocks, 0))
            picked.append(lax.select(slot < n_blocks, near, received[sender]))
        summed = jnp.dot(counts[b], jnp.concatenate(picked, axis=0), preferred_element_type=jnp.float32)
        scale = inverse[b]
        scale = jnp.concatenate([scale] * (width // ROWS), axis=1)
        per_out = n_blocks // len(outs)
        begin = i % per_out * ROWS
        outs[i // per_out][begin : begin + ROWS, :] = (summed * scale).astype(h.dtype)


def aggregate(last, core, tile_src, h, received, counts, inverse):
    rows, width = h.shape
    n_outs = 2 if last else 1
    outs = call(
        functools.partial(aggregate_kernel, last),
        "aggregate",
        (SMEM, SMEM, VMEM, VMEM, VMEM, VMEM),
        [like(h, (rows // n_outs, width // 2))] * n_outs,
        (VMEM,) * n_outs,
    )(core, tile_src, h, received, counts, inverse)
    return outs[0], outs[-1]


def own_products_kernel(layer, core_ref, h, mean_mine, gathered, pre):
    core, width = core_ref[0], h.shape[1]
    parts = gathered[2 * layer, width : width + SPLIT_ROWS, :].astype(jnp.float32)
    bias = ((parts[4:6] + parts[2:4]) + parts[0:2])[0:1]
    right = jnp.concatenate(
        [gathered[2 * layer, 0:width, :], gathered[2 * layer + 1, part(core, width // 2), :]], axis=0
    )
    n_chunks = pre.shape[0] // CHUNK
    for c in range(n_chunks):
        rows = pl.ds(c * CHUNK, CHUNK)
        h_rows = rows if pre.shape[0] == h.shape[0] else part(core * n_chunks + c, CHUNK)
        left = jnp.concatenate([h[h_rows, :], mean_mine[rows, :]], axis=1)
        pre[rows, :] = jnp.dot(left, right, preferred_element_type=jnp.float32) + bias


def own_products(layer, core, h, mean_mine, gathered):
    (out,) = call(
        functools.partial(own_products_kernel, layer),
        "own_products",
        (SMEM, VMEM, VMEM, VMEM),
        [jax.ShapeDtypeStruct((mean_mine.shape[0], h.shape[1]), jnp.float32)],
        (VMEM,),
    )(core, h, mean_mine, gathered)
    return out


def layer_rows(layer, core, c, pre, mean_other, gathered, summed):
    width = pre.shape[1]
    parts = gathered[2 * layer, width : width + SPLIT_ROWS, :].astype(jnp.float32)
    gain = ((parts[4:6] + parts[2:4]) + parts[0:2])[1:2]
    right = gathered[2 * layer + 1, part(1 - core, width // 2), :]
    rows = pl.ds(c * CHUNK, CHUNK)
    summed[...] = pre[rows, :] + jnp.dot(mean_other[rows, :], right, preferred_element_type=jnp.float32)
    for begin in range(0, CHUNK, 64):
        x = summed[begin : begin + 64, :]
        mu = jnp.mean(x, axis=1, keepdims=True)
        centred = x - mu
        var = jnp.mean(centred * centred, axis=1, keepdims=True)
        value = jnp.maximum(centred * lax.rsqrt(var + 1e-05) * gain, 0.0)
        yield c * CHUNK + begin, value.astype(mean_other.dtype)


def dense_kernel(layer, core_ref, blocks, pre, mean_other, gathered, h_out, outgoing, summed):
    core = core_ref[0]
    for c in range(pre.shape[0] // CHUNK):
        for begin, value in layer_rows(layer, core, c, pre, mean_other, gathered, summed.at[c]):
            h_out[begin : begin + 64, :] = value
    for j in range(outgoing.shape[0]):
        outgoing[j] = h_out[block_rows(blocks[reader_of(j)]), part(core, outgoing.shape[2])]


def dense(layer, core, blocks, pre, mean_other, gathered):
    rows, width = pre.shape
    return call(
        functools.partial(dense_kernel, layer),
        "dense",
        (SMEM, SMEM) + (VMEM,) * 3,
        [like(mean_other, pre.shape), like(mean_other, (blocks.shape[0], ROWS, width // 2))],
        (VMEM, VMEM),
        [pltpu.VMEM((rows // CHUNK, CHUNK, width), jnp.float32)],
    )(core, blocks, pre, mean_other, gathered)


def last_dense_kernel(core_ref, pre, mean_other, gathered, *rest):
    *kept, leaving, summed, sems = rest
    core, last = core_ref[0], N_LAYERS - 1
    half_rows = leaving.shape[1]
    copies = [
        pltpu.make_async_copy(source.at[part(core, half_rows)], leaving.at[layer], sems.at[layer])
        for layer, source in enumerate(kept)
    ]
    for copy in copies:
        copy.start()
    for c in range(half_rows // CHUNK):
        for begin, value in layer_rows(last, core, c, pre, mean_other, gathered, summed.at[c]):
            leaving[last, begin : begin + 64, :] = value
    for copy in copies:
        copy.wait()


def last_dense(core, pre, mean_other, gathered, kept):
    half_rows, width = pre.shape
    (out,) = call(
        last_dense_kernel,
        "last_dense",
        (SMEM,) + (VMEM,) * 3 + (HBM,) * len(kept),
        [like(mean_other, (N_LAYERS, half_rows, width))],
        (VMEM,),
        [
            pltpu.VMEM((half_rows // CHUNK, CHUNK, width), jnp.float32),
            pltpu.SemaphoreType.DMA((N_LAYERS - 1,)),
        ],
    )(core, pre, mean_other, gathered, *kept)
    return out


def finish_kernel(crossing, core_ref, source, *rest):
    out, sems = rest[-2:]
    core, chunk = core_ref[0], source.shape[1]
    half = 1 - core if crossing else core
    pieces = []
    for g in range(2):
        piece = source.at[g] if crossing else source.at[2 * g + core]
        pieces.append((piece, out.at[g, part(half, chunk)]))
    run_copies(pieces, sems)


def finish(crossing, core, source, *results):
    _, chunk, width = source.shape
    (out,) = call(
        functools.partial(finish_kernel, crossing),
        "finish",
        (SMEM, VMEM) + (HBM,) * len(results),
        [like(source, (2, 2 * chunk, width))],
        (HBM,),
        [pltpu.SemaphoreType.DMA((2,))],
        input_output_aliases={2: 0} if crossing else {},
    )(core, source, *results)
    return out


def theirs_kernel(core_ref, straight, out, sems):
    core = core_ref[0]
    run_copies([(straight.at[2 * g + 1 - core], out.at[g]) for g in range(2)], sems)


def theirs(core, straight):
    (out,) = call(
        theirs_kernel,
        "theirs",
        (SMEM, VMEM),
        [like(straight, (2,) + straight.shape[1:])],
        (VMEM,),
        [pltpu.SemaphoreType.DMA((2,))],
    )(core, straight)
    return out


def swap(value):
    return lax.ppermute(value, "dc", [(0, 1), (1, 0)])


def scalars(*values):
    return jnp.stack([jnp.asarray(v).astype(jnp.int32) for v in values])


def body(features, w_self, w_neigh, bias, gain, hubs, tile_src, counts):
    graph, parity = lax.axis_index("sm"), lax.axis_index("se")
    core = lax.axis_index("dc")
    section = 2 * graph + parity
    here = core == parity
    n_hubs = hubs.shape[1]
    place = scalars(graph, parity, core)

    outgoing, packed = front(hubs[:, :, 0], features, w_self, w_neigh, bias, gain)
    gathered = lax.all_gather(packed, SECTION + ("dc",))
    received = lax.all_to_all(outgoing, CORES, 0, 0, tiled=True)

    blocks = jnp.maximum(lax.dynamic_index_in_dim(hubs, graph, 0, keepdims=False).reshape(-1), 0)
    lists = jnp.concatenate(
        [blocks, lax.dynamic_index_in_dim(tile_src, graph, 0, keepdims=False).reshape(-1)]
    )
    lists = jnp.where(here, lists, swap(lists))
    blocks, tiles = lists[:n_hubs], lists[n_hubs:]
    counts, outgoing = lax.optimization_barrier((counts, outgoing))
    tile_counts, inverse = tally(place, counts)
    h, tile_counts, inverse = ready(
        place, features, tile_counts, inverse, swap(features), swap(tile_counts), swap(inverse)
    )
    core_ref, kept = scalars(core), []
    for layer in range(N_LAYERS):
        if layer > 0:
            received = lax.all_to_all(outgoing, CHIPS, 0, 0, tiled=True)
        else:
            received, gathered = lax.optimization_barrier((received, gathered))
        last = layer == N_LAYERS - 1
        theirs_too, mean_mine = aggregate(last, core_ref, tiles, h, received, tile_counts, inverse)
        mean_other = swap(theirs_too)
        pre = own_products(layer, core_ref, h, mean_mine, gathered)
        if last:
            leaving = last_dense(core_ref, pre, mean_other, gathered, kept)
        else:
            h, outgoing = dense(layer, core_ref, blocks, pre, mean_other, gathered)
            kept.append(h)
    straight = lax.all_to_all(leaving, SECTION, 0, 0, tiled=True)
    crossed = swap(theirs(core_ref, straight))
    results = finish(True, core_ref, crossed, finish(False, core_ref, straight))
    return results[None]


def solution(mesh):
    n_section, n_dp = mesh.shape["section"], mesh.shape["dp"]
    units = Mesh(mesh.devices.reshape(2, n_section // 2, n_dp // 2 // SIDE, SIDE, 2), SECTION + PARTS)
    placed = (
        P(None, PARTS, None),
        P(SECTION, None, None),
        P(SECTION, None, None),
        P(SECTION, None),
        P(SECTION, None),
        P(None, None, PARTS),
        P(None, PARTS, None),
        P(None, PARTS, None, None, None),
    )
    return jax.shard_map(
        body, mesh=units, in_specs=placed, out_specs=P(SECTION, None, PARTS, None), check_vma=False
    )
```

```python
import functools

import jax
import jax.numpy as jnp
from jax import lax
from jax.experimental import pallas as pl
from jax.experimental.pallas import tpu as pltpu
from jax.sharding import Mesh, PartitionSpec as P

SECTION = ("sm", "se")
PARTS = ("dz", "dx", "dc")
CHIPS, CORES = ("dx", "se", "dz"), ("dx", "dc", "dz")
SIDE = 4
ROWS = 128
CHUNK = 256
N_LAYERS = 4
SPLIT_ROWS = 16
VMEM, SMEM, HBM = pltpu.VMEM, pltpu.SMEM, pltpu.HBM


MIB = 1024 * 1024


def params(mib=24):
    return pltpu.CompilerParams(vmem_limit_bytes=mib * MIB)


def call(kernel, name, in_spaces, out_shape, out_spaces, scratch=(), mib=24, **kwargs):
    return pl.pallas_call(
        kernel,
        out_shape=out_shape,
        in_specs=[pl.BlockSpec(memory_space=s) for s in in_spaces],
        out_specs=[pl.BlockSpec(memory_space=s) for s in out_spaces],
        scratch_shapes=list(scratch),
        compiler_params=params(mib),
        name=name,
        **kwargs,
    )


def like(array, shape=None):
    return jax.ShapeDtypeStruct(shape or array.shape, array.dtype)


def part(index, size):
    return pl.ds(pl.multiple_of(index * size, size), size)


def block_rows(block):
    return part(block, ROWS)


def run_copies(pieces, sems):
    copies = [pltpu.make_async_copy(s, d, sems.at[i]) for i, (s, d) in enumerate(pieces)]
    for copy in copies:
        copy.start()
    for copy in copies:
        copy.wait()


def reader_of(j):
    x, e, z = j // (2 * SIDE), j // SIDE % 2, j % SIDE
    return 2 * (z * SIDE + x) + e


def place_of(partition):
    chip, e = lax.div(partition, 2), lax.rem(partition, 2)
    z, x = lax.div(chip, SIDE), lax.rem(chip, SIDE)
    return x * (2 * SIDE) + e * SIDE + z


def front_kernel(
    hubs, features, w_self, w_neigh, bias, gain, outgoing, packed_out, held, packed, load_sem, w_sem, out_sem, sems
):
    graph, parity, core = lax.axis_index("sm"), lax.axis_index("se"), lax.axis_index("dc")
    width = packed.shape[1]
    load = pltpu.make_async_copy(features.at[graph], held, load_sem)
    load.start()
    for index, source in enumerate((w_self, w_neigh)):

        @pl.when(core == index)
        def _(source=source):
            pltpu.make_async_copy(source.at[0], packed.at[pl.ds(0, width)], w_sem).start()

    values = jnp.concatenate([bias[...], gain[...]], axis=0)
    parts = []
    for _ in range(3):
        part = values.astype(packed.dtype).astype(jnp.float32)
        parts.append(part)
        values = values - part
    parts.append(jnp.zeros((SPLIT_ROWS - 6, width), jnp.float32))
    packed[width : width + SPLIT_ROWS, :] = jnp.concatenate(parts, axis=0).astype(packed.dtype)
    load.wait()
    half = outgoing.shape[2]
    copies = []
    for j in range(outgoing.shape[0]):
        reader = reader_of(j)
        block = jnp.maximum(hubs[graph, reader - reader % 2 + parity], 0)
        source = held.at[block_rows(block), pl.ds((reader % 2) * half, half)]
        copies.append(pltpu.make_async_copy(source, outgoing.at[j], sems.at[j]))
        copies[-1].start()
    pltpu.make_async_copy(w_self.at[0], packed.at[pl.ds(0, width)], w_sem).wait()
    copies.append(pltpu.make_async_copy(packed, packed_out, out_sem))
    copies[-1].start()
    for copy in copies:
        copy.wait()


def front(hubs, features, w_self, w_neigh, bias, gain):
    n_hubs, (_, rows, width) = hubs.shape[1], features.shape
    return call(
        front_kernel,
        "front",
        (SMEM, HBM, HBM, HBM, VMEM, VMEM),
        [like(features, (n_hubs, ROWS, width // 2)), like(w_self, (width + SPLIT_ROWS, width))],
        (HBM, HBM),
        [
            pltpu.VMEM((rows, width), features.dtype),
            pltpu.VMEM((width + SPLIT_ROWS, width), w_self.dtype),
            pltpu.SemaphoreType.DMA,
            pltpu.SemaphoreType.DMA,
            pltpu.SemaphoreType.DMA,
            pltpu.SemaphoreType.DMA((n_hubs,)),
        ],
        mib=56,
    )(hubs, features, w_self, w_neigh, bias, gain)


def ready_kernel(place, *refs):
    sources, (h, counts, inverse, sems) = refs[:6], refs[6:]
    here = place[1] == place[2]
    for held, want in enumerate((jnp.logical_not(here), here)):

        @pl.when(want)
        def _(held=held):
            feats, tile_counts, inverses = sources[3 * (1 - held) : 3 * (1 - held) + 3]
            feats = feats.at[place[0]]
            run_copies([(feats, h), (tile_counts, counts), (inverses, inverse)], sems)


def ready(place, feats, counts, inverse, feats_swapped, counts_swapped, inverse_swapped):
    _, rows, width = feats.shape
    return call(
        ready_kernel,
        "ready",
        (SMEM,) + (HBM,) * 6,
        [like(feats, (rows, width)), like(counts), like(inverse)],
        (VMEM,) * 3,
        [pltpu.SemaphoreType.DMA((3,))],
    )(place, feats, counts, inverse, feats_swapped, counts_swapped, inverse_swapped)


def tally_kernel(place, counts, out, inverse):
    tiles = counts.shape[2]
    total = jnp.zeros((ROWS, ROWS), jnp.float32)
    for j in range(tiles):
        tile = counts[0, 0, j].astype(jnp.float32)
        total = total + tile
        out[0, :, j * ROWS : (j + 1) * ROWS] = tile.astype(out.dtype)
    degree = jnp.sum(total, axis=1, keepdims=True)
    inverse[0] = jnp.broadcast_to(1.0 / jnp.maximum(degree, 1.0), (ROWS, ROWS))


def tally(place, counts):
    n_blocks, tiles = counts.shape[1], counts.shape[2]
    return pl.pallas_call(
        tally_kernel,
        out_shape=[
            jax.ShapeDtypeStruct((n_blocks, ROWS, tiles * ROWS), jnp.bfloat16),
            jax.ShapeDtypeStruct((n_blocks, ROWS, ROWS), jnp.float32),
        ],
        grid_spec=pltpu.PrefetchScalarGridSpec(
            num_scalar_prefetch=1,
            grid=(n_blocks,),
            in_specs=[pl.BlockSpec((1, 1, tiles, ROWS, ROWS), lambda b, place: (place[0], b, 0, 0, 0))],
            out_specs=[
                pl.BlockSpec((1, ROWS, tiles * ROWS), lambda b, place: (b, 0, 0)),
                pl.BlockSpec((1, ROWS, ROWS), lambda b, place: (b, 0, 0)),
            ],
        ),
        compiler_params=params(),
        name="tally",
    )(place, counts)


def aggregate_kernel(last, core_ref, tile_src, h, received, counts, inverse, *outs):
    n_blocks = counts.shape[0]
    tiles = counts.shape[2] // ROWS
    core, width = core_ref[0], outs[0].shape[1]
    cols = part(core, width)
    for i in range(n_blocks):
        b = lax.rem(n_blocks // 2 * (1 - core) + i, n_blocks) if last else i
        picked = []
        for j in range(tiles):
            slot = tile_src[b * tiles + j]
            near = h[block_rows(jnp.minimum(slot, n_blocks - 1)), cols]
            sender = place_of(jnp.maximum(slot - n_blocks, 0))
            picked.append(lax.select(slot < n_blocks, near, received[sender]))
        summed = jnp.dot(counts[b], jnp.concatenate(picked, axis=0), preferred_element_type=jnp.float32)
        scale = inverse[b]
        scale = jnp.concatenate([scale] * (width // ROWS), axis=1)
        per_out = n_blocks // len(outs)
        begin = i % per_out * ROWS
        outs[i // per_out][begin : begin + ROWS, :] = (summed * scale).astype(h.dtype)


def aggregate(last, core, tile_src, h, received, counts, inverse):
    rows, width = h.shape
    n_outs = 2 if last else 1
    outs = call(
        functools.partial(aggregate_kernel, last),
        "aggregate",
        (SMEM, SMEM, VMEM, VMEM, VMEM, VMEM),
        [like(h, (rows // n_outs, width // 2))] * n_outs,
        (VMEM,) * n_outs,
    )(core, tile_src, h, received, counts, inverse)
    return outs[0], outs[-1]


def own_products_kernel(layer, core_ref, h, mean_mine, gathered, pre):
    core, width = core_ref[0], h.shape[1]
    parts = gathered[2 * layer, width : width + SPLIT_ROWS, :].astype(jnp.float32)
    bias = ((parts[4:6] + parts[2:4]) + parts[0:2])[0:1]
    right = jnp.concatenate(
        [gathered[2 * layer, 0:width, :], gathered[2 * layer + 1, part(core, width // 2), :]], axis=0
    )
    n_chunks = pre.shape[0] // CHUNK
    for c in range(n_chunks):
        rows = pl.ds(c * CHUNK, CHUNK)
        h_rows = rows if pre.shape[0] == h.shape[0] else part(core * n_chunks + c, CHUNK)
        left = jnp.concatenate([h[h_rows, :], mean_mine[rows, :]], axis=1)
        pre[rows, :] = jnp.dot(left, right, preferred_element_type=jnp.float32) + bias


def own_products(layer, core, h, mean_mine, gathered):
    (out,) = call(
        functools.partial(own_products_kernel, layer),
        "own_products",
        (SMEM, VMEM, VMEM, VMEM),
        [jax.ShapeDtypeStruct((mean_mine.shape[0], h.shape[1]), jnp.float32)],
        (VMEM,),
    )(core, h, mean_mine, gathered)
    return out


def layer_rows(layer, core, c, pre, mean_other, gathered, summed):
    width = pre.shape[1]
    parts = gathered[2 * layer, width : width + SPLIT_ROWS, :].astype(jnp.float32)
    gain = ((parts[4:6] + parts[2:4]) + parts[0:2])[1:2]
    right = gathered[2 * layer + 1, part(1 - core, width // 2), :]
    rows = pl.ds(c * CHUNK, CHUNK)
    summed[...] = pre[rows, :] + jnp.dot(mean_other[rows, :], right, preferred_element_type=jnp.float32)
    for begin in range(0, CHUNK, 64):
        x = summed[begin : begin + 64, :]
        mu = jnp.mean(x, axis=1, keepdims=True)
        centred = x - mu
        var = jnp.mean(centred * centred, axis=1, keepdims=True)
        value = jnp.maximum(centred * lax.rsqrt(var + 1e-05) * gain, 0.0)
        yield c * CHUNK + begin, value.astype(mean_other.dtype)


def dense_kernel(layer, core_ref, blocks, pre, mean_other, gathered, h_out, outgoing, summed):
    core = core_ref[0]
    for c in range(pre.shape[0] // CHUNK):
        for begin, value in layer_rows(layer, core, c, pre, mean_other, gathered, summed.at[c]):
            h_out[begin : begin + 64, :] = value
    for j in range(outgoing.shape[0]):
        outgoing[j] = h_out[block_rows(blocks[reader_of(j)]), part(core, outgoing.shape[2])]


def dense(layer, core, blocks, pre, mean_other, gathered):
    rows, width = pre.shape
    return call(
        functools.partial(dense_kernel, layer),
        "dense",
        (SMEM, SMEM) + (VMEM,) * 3,
        [like(mean_other, pre.shape), like(mean_other, (blocks.shape[0], ROWS, width // 2))],
        (VMEM, VMEM),
        [pltpu.VMEM((rows // CHUNK, CHUNK, width), jnp.float32)],
    )(core, blocks, pre, mean_other, gathered)


def last_dense_kernel(core_ref, pre, mean_other, gathered, *rest):
    *kept, leaving, summed, sems = rest
    core, last = core_ref[0], N_LAYERS - 1
    half_rows = leaving.shape[1]
    copies = [
        pltpu.make_async_copy(source.at[part(core, half_rows)], leaving.at[layer], sems.at[layer])
        for layer, source in enumerate(kept)
    ]
    for copy in copies:
        copy.start()
    for c in range(half_rows // CHUNK):
        for begin, value in layer_rows(last, core, c, pre, mean_other, gathered, summed.at[c]):
            leaving[last, begin : begin + 64, :] = value
    for copy in copies:
        copy.wait()


def last_dense(core, pre, mean_other, gathered, kept):
    half_rows, width = pre.shape
    (out,) = call(
        last_dense_kernel,
        "last_dense",
        (SMEM,) + (VMEM,) * 3 + (HBM,) * len(kept),
        [like(mean_other, (N_LAYERS, half_rows, width))],
        (VMEM,),
        [
            pltpu.VMEM((half_rows // CHUNK, CHUNK, width), jnp.float32),
            pltpu.SemaphoreType.DMA((N_LAYERS - 1,)),
        ],
    )(core, pre, mean_other, gathered, *kept)
    return out


def finish_kernel(crossing, core_ref, source, *rest):
    out, sems = rest[-2:]
    core, chunk = core_ref[0], source.shape[1]
    half = 1 - core if crossing else core
    pieces = []
    for g in range(2):
        piece = source.at[g] if crossing else source.at[2 * g + core]
        pieces.append((piece, out.at[g, part(half, chunk)]))
    run_copies(pieces, sems)


def finish(crossing, core, source, *results):
    _, chunk, width = source.shape
    (out,) = call(
        functools.partial(finish_kernel, crossing),
        "finish",
        (SMEM, VMEM) + (HBM,) * len(results),
        [like(source, (2, 2 * chunk, width))],
        (HBM,),
        [pltpu.SemaphoreType.DMA((2,))],
        input_output_aliases={2: 0} if crossing else {},
    )(core, source, *results)
    return out


def theirs_kernel(core_ref, straight, out, sems):
    core = core_ref[0]
    run_copies([(straight.at[2 * g + 1 - core], out.at[g]) for g in range(2)], sems)


def theirs(core, straight):
    (out,) = call(
        theirs_kernel,
        "theirs",
        (SMEM, VMEM),
        [like(straight, (2,) + straight.shape[1:])],
        (VMEM,),
        [pltpu.SemaphoreType.DMA((2,))],
    )(core, straight)
    return out


def swap(value):
    return lax.ppermute(value, "dc", [(0, 1), (1, 0)])


def scalars(*values):
    return jnp.stack([jnp.asarray(v).astype(jnp.int32) for v in values])


def body(features, w_self, w_neigh, bias, gain, hubs, tile_src, counts):
    graph, parity = lax.axis_index("sm"), lax.axis_index("se")
    core = lax.axis_index("dc")
    section = 2 * graph + parity
    here = core == parity
    n_hubs = hubs.shape[1]
    place = scalars(graph, parity, core)

    outgoing, packed = front(hubs[:, :, 0], features, w_self, w_neigh, bias, gain)
    gathered = lax.all_gather(packed, SECTION + ("dc",))
    received = lax.all_to_all(outgoing, CORES, 0, 0, tiled=True)

    blocks = jnp.maximum(lax.dynamic_index_in_dim(hubs, graph, 0, keepdims=False).reshape(-1), 0)
    lists = jnp.concatenate(
        [blocks, lax.dynamic_index_in_dim(tile_src, graph, 0, keepdims=False).reshape(-1)]
    )
    lists = jnp.where(here, lists, swap(lists))
    blocks, tiles = lists[:n_hubs], lists[n_hubs:]
    counts, outgoing = lax.optimization_barrier((counts, outgoing))
    tile_counts, inverse = tally(place, counts)
    h, tile_counts, inverse = ready(
        place, features, tile_counts, inverse, swap(features), swap(tile_counts), swap(inverse)
    )
    core_ref, kept = scalars(core), []
    for layer in range(N_LAYERS):
        if layer > 0:
            received = lax.all_to_all(outgoing, CHIPS, 0, 0, tiled=True)
        else:
            received, gathered = lax.optimization_barrier((received, gathered))
        last = layer == N_LAYERS - 1
        theirs_too, mean_mine = aggregate(last, core_ref, tiles, h, received, tile_counts, inverse)
        mean_other = swap(theirs_too)
        pre = own_products(layer, core_ref, h, mean_mine, gathered)
        if last:
            leaving = last_dense(core_ref, pre, mean_other, gathered, kept)
        else:
            h, outgoing = dense(layer, core_ref, blocks, pre, mean_other, gathered)
            kept.append(h)
    straight = lax.all_to_all(leaving, SECTION, 0, 0, tiled=True)
    crossed = swap(theirs(core_ref, straight))
    results = finish(True, core_ref, crossed, finish(False, core_ref, straight))
    return results[None]


def solution(mesh):
    n_section, n_dp = mesh.shape["section"], mesh.shape["dp"]
    units = Mesh(mesh.devices.reshape(2, n_section // 2, n_dp // 2 // SIDE, SIDE, 2), SECTION + PARTS)
    placed = (
        P(None, PARTS, None),
        P(SECTION, None, None),
        P(SECTION, None, None),
        P(SECTION, None),
        P(SECTION, None),
        P(None, None, PARTS),
        P(None, PARTS, None),
        P(None, PARTS, None, None, None),
    )
    return jax.shard_map(
        body, mesh=units, in_specs=placed, out_specs=P(SECTION, None, PARTS, None), check_vma=False
    )
```

```python
import functools

import jax
import jax.numpy as jnp
from jax import lax
from jax.experimental import pallas as pl
from jax.experimental.pallas import tpu as pltpu
from jax.sharding import Mesh, PartitionSpec as P

SECTION = ("sm", "se")
PARTS = ("dz", "dx", "dc")
CHIPS, CORES = ("dx", "se", "dz"), ("dx", "dc", "dz")
SIDE = 4
ROWS = 128
CHUNK = 256
N_LAYERS = 4
SPLIT_ROWS = 16
VMEM, SMEM, HBM = pltpu.VMEM, pltpu.SMEM, pltpu.HBM


MIB = 1024 * 1024


def params(mib=24):
    return pltpu.CompilerParams(vmem_limit_bytes=mib * MIB)


def call(kernel, name, in_spaces, out_shape, out_spaces, scratch=(), mib=24, **kwargs):
    return pl.pallas_call(
        kernel,
        out_shape=out_shape,
        in_specs=[pl.BlockSpec(memory_space=s) for s in in_spaces],
        out_specs=[pl.BlockSpec(memory_space=s) for s in out_spaces],
        scratch_shapes=list(scratch),
        compiler_params=params(mib),
        name=name,
        **kwargs,
    )


def like(array, shape=None):
    return jax.ShapeDtypeStruct(shape or array.shape, array.dtype)


def part(index, size):
    return pl.ds(pl.multiple_of(index * size, size), size)


def block_rows(block):
    return part(block, ROWS)


def run_copies(pieces, sems):
    copies = [pltpu.make_async_copy(s, d, sems.at[i]) for i, (s, d) in enumerate(pieces)]
    for copy in copies:
        copy.start()
    for copy in copies:
        copy.wait()


def reader_of(j):
    x, e, z = j // (2 * SIDE), j // SIDE % 2, j % SIDE
    return 2 * (z * SIDE + x) + e


def place_of(partition):
    chip, e = lax.div(partition, 2), lax.rem(partition, 2)
    z, x = lax.div(chip, SIDE), lax.rem(chip, SIDE)
    return x * (2 * SIDE) + e * SIDE + z


def front_kernel(
    hubs, features, w_self, w_neigh, bias, gain, outgoing, packed_out, held, packed, load_sem, w_sem, out_sem, sems
):
    graph, parity, core = lax.axis_index("sm"), lax.axis_index("se"), lax.axis_index("dc")
    width = packed.shape[1]
    load = pltpu.make_async_copy(features.at[graph], held, load_sem)
    load.start()
    for index, source in enumerate((w_self, w_neigh)):

        @pl.when(core == index)
        def _(source=source):
            pltpu.make_async_copy(source.at[0], packed.at[pl.ds(0, width)], w_sem).start()

    values = jnp.concatenate([bias[...], gain[...]], axis=0)
    parts = []
    for _ in range(3):
        part = values.astype(packed.dtype).astype(jnp.float32)
        parts.append(part)
        values = values - part
    parts.append(jnp.zeros((SPLIT_ROWS - 6, width), jnp.float32))
    packed[width : width + SPLIT_ROWS, :] = jnp.concatenate(parts, axis=0).astype(packed.dtype)
    load.wait()
    half = outgoing.shape[2]
    copies = []
    for j in range(outgoing.shape[0]):
        reader = reader_of(j)
        block = jnp.maximum(hubs[graph, reader - reader % 2 + parity], 0)
        source = held.at[block_rows(block), pl.ds((reader % 2) * half, half)]
        copies.append(pltpu.make_async_copy(source, outgoing.at[j], sems.at[j]))
        copies[-1].start()
    pltpu.make_async_copy(w_self.at[0], packed.at[pl.ds(0, width)], w_sem).wait()
    copies.append(pltpu.make_async_copy(packed, packed_out, out_sem))
    copies[-1].start()
    for copy in copies:
        copy.wait()


def front(hubs, features, w_self, w_neigh, bias, gain):
    n_hubs, (_, rows, width) = hubs.shape[1], features.shape
    return call(
        front_kernel,
        "front",
        (SMEM, HBM, HBM, HBM, VMEM, VMEM),
        [like(features, (n_hubs, ROWS, width // 2)), like(w_self, (width + SPLIT_ROWS, width))],
        (HBM, HBM),
        [
            pltpu.VMEM((rows, width), features.dtype),
            pltpu.VMEM((width + SPLIT_ROWS, width), w_self.dtype),
            pltpu.SemaphoreType.DMA,
            pltpu.SemaphoreType.DMA,
            pltpu.SemaphoreType.DMA,
            pltpu.SemaphoreType.DMA((n_hubs,)),
        ],
        mib=56,
    )(hubs, features, w_self, w_neigh, bias, gain)


def ready_kernel(place, *refs):
    sources, (h, counts, inverse, sems) = refs[:6], refs[6:]
    here = place[1] == place[2]
    for held, want in enumerate((jnp.logical_not(here), here)):

        @pl.when(want)
        def _(held=held):
            feats, tile_counts, inverses = sources[3 * (1 - held) : 3 * (1 - held) + 3]
            feats = feats.at[place[0]]
            run_copies([(feats, h), (tile_counts, counts), (inverses, inverse)], sems)


def ready(place, feats, counts, inverse, feats_swapped, counts_swapped, inverse_swapped):
    _, rows, width = feats.shape
    return call(
        ready_kernel,
        "ready",
        (SMEM,) + (HBM,) * 6,
        [like(feats, (rows, width)), like(counts), like(inverse)],
        (VMEM,) * 3,
        [pltpu.SemaphoreType.DMA((3,))],
    )(place, feats, counts, inverse, feats_swapped, counts_swapped, inverse_swapped)


def tally_kernel(place, counts, out, inverse):
    tiles = counts.shape[2]
    total = jnp.zeros((ROWS, ROWS), jnp.float32)
    for j in range(tiles):
        tile = counts[0, 0, j].astype(jnp.float32)
        total = total + tile
        out[0, :, j * ROWS : (j + 1) * ROWS] = tile.astype(out.dtype)
    degree = jnp.sum(total, axis=1, keepdims=True)
    inverse[0] = jnp.broadcast_to(1.0 / jnp.maximum(degree, 1.0), (ROWS, ROWS))


def tally(place, counts):
    n_blocks, tiles = counts.shape[1], counts.shape[2]
    return pl.pallas_call(
        tally_kernel,
        out_shape=[
            jax.ShapeDtypeStruct((n_blocks, ROWS, tiles * ROWS), jnp.bfloat16),
            jax.ShapeDtypeStruct((n_blocks, ROWS, ROWS), jnp.float32),
        ],
        grid_spec=pltpu.PrefetchScalarGridSpec(
            num_scalar_prefetch=1,
            grid=(n_blocks,),
            in_specs=[pl.BlockSpec((1, 1, tiles, ROWS, ROWS), lambda b, place: (place[0], b, 0, 0, 0))],
            out_specs=[
                pl.BlockSpec((1, ROWS, tiles * ROWS), lambda b, place: (b, 0, 0)),
                pl.BlockSpec((1, ROWS, ROWS), lambda b, place: (b, 0, 0)),
            ],
        ),
        compiler_params=params(),
        name="tally",
    )(place, counts)


def aggregate_kernel(last, tile_src, h, received, counts, inverse, *outs):
    n_blocks = counts.shape[0]
    tiles = counts.shape[2] // ROWS
    core, width = lax.axis_index("dc"), outs[0].shape[1]
    cols = part(core, width)
    for i in range(n_blocks):
        b = lax.rem(n_blocks // 2 * (1 - core) + i, n_blocks) if last else i
        picked = []
        for j in range(tiles):
            slot = tile_src[b * tiles + j]
            near = h[block_rows(jnp.minimum(slot, n_blocks - 1)), cols]
            sender = place_of(jnp.maximum(slot - n_blocks, 0))
            picked.append(lax.select(slot < n_blocks, near, received[sender]))
        summed = jnp.dot(counts[b], jnp.concatenate(picked, axis=0), preferred_element_type=jnp.float32)
        scale = inverse[b]
        scale = jnp.concatenate([scale] * (width // ROWS), axis=1)
        per_out = n_blocks // len(outs)
        begin = i % per_out * ROWS
        outs[i // per_out][begin : begin + ROWS, :] = (summed * scale).astype(h.dtype)


def aggregate(last, tile_src, h, received, counts, inverse):
    rows, width = h.shape
    n_outs = 2 if last else 1
    outs = call(
        functools.partial(aggregate_kernel, last),
        "aggregate",
        (SMEM, VMEM, VMEM, VMEM, VMEM),
        [like(h, (rows // n_outs, width // 2))] * n_outs,
        (VMEM,) * n_outs,
    )(tile_src, h, received, counts, inverse)
    return outs[0], outs[-1]


def own_products_kernel(layer, h, mean_mine, gathered, pre):
    core, width = lax.axis_index("dc"), h.shape[1]
    parts = gathered[2 * layer, width : width + SPLIT_ROWS, :].astype(jnp.float32)
    bias = ((parts[4:6] + parts[2:4]) + parts[0:2])[0:1]
    right = jnp.concatenate(
        [gathered[2 * layer, 0:width, :], gathered[2 * layer + 1, part(core, width // 2), :]], axis=0
    )
    n_chunks = pre.shape[0] // CHUNK
    for c in range(n_chunks):
        rows = pl.ds(c * CHUNK, CHUNK)
        h_rows = rows if pre.shape[0] == h.shape[0] else part(core * n_chunks + c, CHUNK)
        left = jnp.concatenate([h[h_rows, :], mean_mine[rows, :]], axis=1)
        pre[rows, :] = jnp.dot(left, right, preferred_element_type=jnp.float32) + bias


def own_products(layer, h, mean_mine, gathered):
    (out,) = call(
        functools.partial(own_products_kernel, layer),
        "own_products",
        (VMEM, VMEM, VMEM),
        [jax.ShapeDtypeStruct((mean_mine.shape[0], h.shape[1]), jnp.float32)],
        (VMEM,),
    )(h, mean_mine, gathered)
    return out


def layer_rows(layer, core, c, pre, mean_other, gathered, summed):
    width = pre.shape[1]
    parts = gathered[2 * layer, width : width + SPLIT_ROWS, :].astype(jnp.float32)
    gain = ((parts[4:6] + parts[2:4]) + parts[0:2])[1:2]
    right = gathered[2 * layer + 1, part(1 - core, width // 2), :]
    rows = pl.ds(c * CHUNK, CHUNK)
    summed[...] = pre[rows, :] + jnp.dot(mean_other[rows, :], right, preferred_element_type=jnp.float32)
    for begin in range(0, CHUNK, 128):
        x = summed[begin : begin + 128, :]
        mu = jnp.mean(x, axis=1, keepdims=True)
        centred = x - mu
        var = jnp.mean(centred * centred, axis=1, keepdims=True)
        value = jnp.maximum(centred * lax.rsqrt(var + 1e-05) * gain, 0.0)
        yield c * CHUNK + begin, value.astype(mean_other.dtype)


def dense_kernel(layer, blocks, pre, mean_other, gathered, h_out, outgoing, summed):
    core = lax.axis_index("dc")
    for c in range(pre.shape[0] // CHUNK):
        for begin, value in layer_rows(layer, core, c, pre, mean_other, gathered, summed.at[c]):
            h_out[begin : begin + 128, :] = value
    for j in range(outgoing.shape[0]):
        outgoing[j] = h_out[block_rows(blocks[reader_of(j)]), part(core, outgoing.shape[2])]


def dense(layer, blocks, pre, mean_other, gathered):
    rows, width = pre.shape
    return call(
        functools.partial(dense_kernel, layer),
        "dense",
        (SMEM,) + (VMEM,) * 3,
        [like(mean_other, pre.shape), like(mean_other, (blocks.shape[0], ROWS, width // 2))],
        (VMEM, VMEM),
        [pltpu.VMEM((rows // CHUNK, CHUNK, width), jnp.float32)],
    )(blocks, pre, mean_other, gathered)


def last_dense_kernel(pre, mean_other, gathered, *rest):
    *kept, leaving, summed, sems = rest
    core, last = lax.axis_index("dc"), N_LAYERS - 1
    half_rows = leaving.shape[1]
    copies = [
        pltpu.make_async_copy(source.at[part(core, half_rows)], leaving.at[ring_place(layer)], sems.at[layer])
        for layer, source in enumerate(kept)
    ]
    for copy in copies:
        copy.start()
    for c in range(half_rows // CHUNK):
        for begin, value in layer_rows(last, core, c, pre, mean_other, gathered, summed.at[c]):
            leaving[ring_place(last), begin : begin + 128, :] = value
    for copy in copies:
        copy.wait()


def last_dense(pre, mean_other, gathered, kept):
    half_rows, width = pre.shape
    (out,) = call(
        last_dense_kernel,
        "last_dense",
        (VMEM,) * 3 + (HBM,) * len(kept),
        [like(mean_other, (N_LAYERS, half_rows, width))],
        (VMEM,),
        [
            pltpu.VMEM((half_rows // CHUNK, CHUNK, width), jnp.float32),
            pltpu.SemaphoreType.DMA((N_LAYERS - 1,)),
        ],
    )(pre, mean_other, gathered, *kept)
    return out


def finish_kernel(crossing, source, *rest):
    out, sems = rest[-2:]
    core, chunk = lax.axis_index("dc"), source.shape[1]
    half = 1 - core if crossing else core
    pieces = []
    for g in range(2):
        piece = source.at[g] if crossing else source.at[2 * core + g]
        pieces.append((piece, out.at[g, part(half, chunk)]))
    run_copies(pieces, sems)


def finish(crossing, source, *results):
    _, chunk, width = source.shape
    (out,) = call(
        functools.partial(finish_kernel, crossing),
        "finish",
        (VMEM,) + (HBM,) * len(results),
        [like(source, (2, 2 * chunk, width))],
        (HBM,),
        [pltpu.SemaphoreType.DMA((2,))],
        input_output_aliases={1: 0} if crossing else {},
    )(source, *results)
    return out


def ring_place(section):
    return section % 2 * 2 + section // 2


def theirs_kernel(straight, out, sems):
    core = lax.axis_index("dc")
    run_copies([(straight.at[pl.ds(2 * (1 - core), 2)], out)], sems)


def theirs(straight):
    (out,) = call(
        theirs_kernel,
        "theirs",
        (VMEM,),
        [like(straight, (2,) + straight.shape[1:])],
        (VMEM,),
        [pltpu.SemaphoreType.DMA((2,))],
    )(straight)
    return out


def swap(value):
    return lax.ppermute(value, "dc", [(0, 1), (1, 0)])


def scalars(*values):
    return jnp.stack([jnp.asarray(v).astype(jnp.int32) for v in values])


def body(features, w_self, w_neigh, bias, gain, hubs, tile_src, counts):
    graph, parity = lax.axis_index("sm"), lax.axis_index("se")
    core = lax.axis_index("dc")
    section = 2 * graph + parity
    here = core == parity
    n_hubs = hubs.shape[1]
    place = scalars(graph, parity, core)

    outgoing, packed = front(hubs[:, :, 0], features, w_self, w_neigh, bias, gain)
    gathered = lax.all_gather(packed, SECTION + ("dc",))
    received = lax.all_to_all(outgoing, CORES, 0, 0, tiled=True)

    blocks = jnp.maximum(lax.dynamic_index_in_dim(hubs, graph, 0, keepdims=False).reshape(-1), 0)
    lists = jnp.concatenate(
        [blocks, lax.dynamic_index_in_dim(tile_src, graph, 0, keepdims=False).reshape(-1)]
    )
    lists = jnp.where(here, lists, swap(lists))
    blocks, tiles = lists[:n_hubs], lists[n_hubs:]
    counts, outgoing = lax.optimization_barrier((counts, outgoing))
    tile_counts, inverse = tally(place, counts)
    h, tile_counts, inverse = ready(
        place, features, tile_counts, inverse, swap(features), swap(tile_counts), swap(inverse)
    )
    kept = []
    for layer in range(N_LAYERS):
        if layer > 0:
            received = lax.all_to_all(outgoing, CHIPS, 0, 0, tiled=True)
        else:
            received, gathered = lax.optimization_barrier((received, gathered))
        last = layer == N_LAYERS - 1
        theirs_too, mean_mine = aggregate(last, tiles, h, received, tile_counts, inverse)
        mean_other = swap(theirs_too)
        pre = own_products(layer, h, mean_mine, gathered)
        if last:
            leaving = last_dense(pre, mean_other, gathered, kept)
        else:
            h, outgoing = dense(layer, blocks, pre, mean_other, gathered)
            kept.append(h)
    straight = lax.all_to_all(leaving, ("se", "sm"), 0, 0, tiled=True)
    crossed = swap(theirs(straight))
    results = finish(True, crossed, finish(False, straight))
    return results[None]


def solution(mesh):
    n_section, n_dp = mesh.shape["section"], mesh.shape["dp"]
    units = Mesh(mesh.devices.reshape(2, n_section // 2, n_dp // 2 // SIDE, SIDE, 2), SECTION + PARTS)
    placed = (
        P(None, PARTS, None),
        P(SECTION, None, None),
        P(SECTION, None, None),
        P(SECTION, None),
        P(SECTION, None),
        P(None, None, PARTS),
        P(None, PARTS, None),
        P(None, PARTS, None, None, None),
    )
    return jax.shard_map(
        body, mesh=units, in_specs=placed, out_specs=P(SECTION, None, PARTS, None), check_vma=False
    )
```

```python
import functools

import jax
import jax.numpy as jnp
from jax import lax
from jax.experimental import pallas as pl
from jax.experimental.pallas import tpu as pltpu
from jax.sharding import Mesh, PartitionSpec as P

SECTION = ("sm", "se")
PARTS = ("dz", "dx", "dc")
CHIPS, CORES = ("dx", "se", "dz"), ("dx", "dc", "dz")
SIDE = 4
ROWS = 128
CHUNK = 256
N_LAYERS = 4
SPLIT_ROWS = 16
VMEM, SMEM, HBM = pltpu.VMEM, pltpu.SMEM, pltpu.HBM


MIB = 1024 * 1024


def params(mib=24):
    return pltpu.CompilerParams(vmem_limit_bytes=mib * MIB)


def call(kernel, name, in_spaces, out_shape, out_spaces, scratch=(), mib=24, **kwargs):
    return pl.pallas_call(
        kernel,
        out_shape=out_shape,
        in_specs=[pl.BlockSpec(memory_space=s) for s in in_spaces],
        out_specs=[pl.BlockSpec(memory_space=s) for s in out_spaces],
        scratch_shapes=list(scratch),
        compiler_params=params(mib),
        name=name,
        **kwargs,
    )


def like(array, shape=None):
    return jax.ShapeDtypeStruct(shape or array.shape, array.dtype)


def part(index, size):
    return pl.ds(pl.multiple_of(index * size, size), size)


def block_rows(block):
    return part(block, ROWS)


def run_copies(pieces, sems):
    copies = [pltpu.make_async_copy(s, d, sems.at[i]) for i, (s, d) in enumerate(pieces)]
    for copy in copies:
        copy.start()
    for copy in copies:
        copy.wait()


def reader_of(j):
    x, e, z = j // (2 * SIDE), j // SIDE % 2, j % SIDE
    return 2 * (z * SIDE + x) + e


def place_of(partition):
    chip, e = lax.div(partition, 2), lax.rem(partition, 2)
    z, x = lax.div(chip, SIDE), lax.rem(chip, SIDE)
    return x * (2 * SIDE) + e * SIDE + z


def front_kernel(
    hubs, features, w_self, w_neigh, bias, gain, outgoing, packed_out, held, packed, load_sems, w_sem, out_sem, sems
):
    graph, parity, core = lax.axis_index("sm"), lax.axis_index("se"), lax.axis_index("dc")
    width = packed.shape[1]
    n_loads = load_sems.shape[0]
    step = held.shape[0] // n_loads
    loads = []
    for i in range(n_loads):
        rows = pl.ds(i * step, step)
        loads.append(pltpu.make_async_copy(features.at[graph, rows], held.at[rows], load_sems.at[i]))
        loads[-1].start()
    for index, source in enumerate((w_self, w_neigh)):

        @pl.when(core == index)
        def _(source=source):
            pltpu.make_async_copy(source.at[0], packed.at[pl.ds(0, width)], w_sem).start()

    values = jnp.concatenate([bias[...], gain[...]], axis=0)
    parts = []
    for _ in range(3):
        part = values.astype(packed.dtype).astype(jnp.float32)
        parts.append(part)
        values = values - part
    parts.append(jnp.zeros((SPLIT_ROWS - 6, width), jnp.float32))
    packed[width : width + SPLIT_ROWS, :] = jnp.concatenate(parts, axis=0).astype(packed.dtype)
    for load in loads:
        load.wait()
    half = outgoing.shape[2]
    copies = []
    for j in range(outgoing.shape[0]):
        reader = reader_of(j)
        block = jnp.maximum(hubs[graph, reader - reader % 2 + parity], 0)
        source = held.at[block_rows(block), pl.ds((reader % 2) * half, half)]
        copies.append(pltpu.make_async_copy(source, outgoing.at[j], sems.at[j]))
        copies[-1].start()
    pltpu.make_async_copy(w_self.at[0], packed.at[pl.ds(0, width)], w_sem).wait()
    copies.append(pltpu.make_async_copy(packed, packed_out, out_sem))
    copies[-1].start()
    for copy in copies:
        copy.wait()


def front(hubs, features, w_self, w_neigh, bias, gain):
    n_hubs, (_, rows, width) = hubs.shape[1], features.shape
    return call(
        front_kernel,
        "front",
        (SMEM, HBM, HBM, HBM, VMEM, VMEM),
        [like(features, (n_hubs, ROWS, width // 2)), like(w_self, (width + SPLIT_ROWS, width))],
        (HBM, HBM),
        [
            pltpu.VMEM((rows, width), features.dtype),
            pltpu.VMEM((width + SPLIT_ROWS, width), w_self.dtype),
            pltpu.SemaphoreType.DMA((4,)),
            pltpu.SemaphoreType.DMA,
            pltpu.SemaphoreType.DMA,
            pltpu.SemaphoreType.DMA((n_hubs,)),
        ],
        mib=56,
    )(hubs, features, w_self, w_neigh, bias, gain)


def ready_kernel(place, *refs):
    sources, (h, counts, inverse, sems) = refs[:6], refs[6:]
    here = place[1] == place[2]
    for held, want in enumerate((jnp.logical_not(here), here)):

        @pl.when(want)
        def _(held=held):
            feats, tile_counts, inverses = sources[3 * (1 - held) : 3 * (1 - held) + 3]
            feats = feats.at[place[0]]
            run_copies([(feats, h), (tile_counts, counts), (inverses, inverse)], sems)


def ready(place, feats, counts, inverse, feats_swapped, counts_swapped, inverse_swapped):
    _, rows, width = feats.shape
    return call(
        ready_kernel,
        "ready",
        (SMEM,) + (HBM,) * 6,
        [like(feats, (rows, width)), like(counts), like(inverse)],
        (VMEM,) * 3,
        [pltpu.SemaphoreType.DMA((3,))],
    )(place, feats, counts, inverse, feats_swapped, counts_swapped, inverse_swapped)


def tally_kernel(place, counts, out, inverse):
    tiles = counts.shape[2]
    total = jnp.zeros((ROWS, ROWS), jnp.float32)
    for j in range(tiles):
        tile = counts[0, 0, j].astype(jnp.float32)
        total = total + tile
        out[0, :, j * ROWS : (j + 1) * ROWS] = tile.astype(out.dtype)
    degree = jnp.sum(total, axis=1, keepdims=True)
    inverse[0] = jnp.broadcast_to(1.0 / jnp.maximum(degree, 1.0), (ROWS, ROWS))


def tally(place, counts):
    n_blocks, tiles = counts.shape[1], counts.shape[2]
    return pl.pallas_call(
        tally_kernel,
        out_shape=[
            jax.ShapeDtypeStruct((n_blocks, ROWS, tiles * ROWS), jnp.bfloat16),
            jax.ShapeDtypeStruct((n_blocks, ROWS, ROWS), jnp.float32),
        ],
        grid_spec=pltpu.PrefetchScalarGridSpec(
            num_scalar_prefetch=1,
            grid=(n_blocks,),
            in_specs=[pl.BlockSpec((1, 1, tiles, ROWS, ROWS), lambda b, place: (place[0], b, 0, 0, 0))],
            out_specs=[
                pl.BlockSpec((1, ROWS, tiles * ROWS), lambda b, place: (b, 0, 0)),
                pl.BlockSpec((1, ROWS, ROWS), lambda b, place: (b, 0, 0)),
            ],
        ),
        compiler_params=params(),
        name="tally",
    )(place, counts)


def aggregate_kernel(last, tile_src, h, received, counts, inverse, *outs):
    n_blocks = counts.shape[0]
    tiles = counts.shape[2] // ROWS
    core, width = lax.axis_index("dc"), outs[0].shape[1]
    cols = part(core, width)
    for i in range(n_blocks):
        b = lax.rem(n_blocks // 2 * (1 - core) + i, n_blocks) if last else i
        picked = []
        for j in range(tiles):
            slot = tile_src[b * tiles + j]
            near = h[block_rows(jnp.minimum(slot, n_blocks - 1)), cols]
            sender = place_of(jnp.maximum(slot - n_blocks, 0))
            picked.append(lax.select(slot < n_blocks, near, received[sender]))
        summed = jnp.dot(counts[b], jnp.concatenate(picked, axis=0), preferred_element_type=jnp.float32)
        scale = inverse[b]
        scale = jnp.concatenate([scale] * (width // ROWS), axis=1)
        per_out = n_blocks // len(outs)
        begin = i % per_out * ROWS
        outs[i // per_out][begin : begin + ROWS, :] = (summed * scale).astype(h.dtype)


def aggregate(last, tile_src, h, received, counts, inverse):
    rows, width = h.shape
    n_outs = 2 if last else 1
    outs = call(
        functools.partial(aggregate_kernel, last),
        "aggregate",
        (SMEM, VMEM, VMEM, VMEM, VMEM),
        [like(h, (rows // n_outs, width // 2))] * n_outs,
        (VMEM,) * n_outs,
    )(tile_src, h, received, counts, inverse)
    return outs[0], outs[-1]


def own_products_kernel(layer, h, mean_mine, gathered, pre):
    core, width = lax.axis_index("dc"), h.shape[1]
    parts = gathered[2 * layer, width : width + SPLIT_ROWS, :].astype(jnp.float32)
    bias = ((parts[4:6] + parts[2:4]) + parts[0:2])[0:1]
    right = jnp.concatenate(
        [gathered[2 * layer, 0:width, :], gathered[2 * layer + 1, part(core, width // 2), :]], axis=0
    )
    n_chunks = pre.shape[0] // CHUNK
    for c in range(n_chunks):
        rows = pl.ds(c * CHUNK, CHUNK)
        h_rows = rows if pre.shape[0] == h.shape[0] else part(core * n_chunks + c, CHUNK)
        left = jnp.concatenate([h[h_rows, :], mean_mine[rows, :]], axis=1)
        pre[rows, :] = jnp.dot(left, right, preferred_element_type=jnp.float32) + bias


def own_products(layer, h, mean_mine, gathered):
    (out,) = call(
        functools.partial(own_products_kernel, layer),
        "own_products",
        (VMEM, VMEM, VMEM),
        [jax.ShapeDtypeStruct((mean_mine.shape[0], h.shape[1]), jnp.float32)],
        (VMEM,),
    )(h, mean_mine, gathered)
    return out


def layer_rows(layer, core, c, pre, mean_other, gathered, summed):
    width = pre.shape[1]
    parts = gathered[2 * layer, width : width + SPLIT_ROWS, :].astype(jnp.float32)
    gain = ((parts[4:6] + parts[2:4]) + parts[0:2])[1:2]
    right = gathered[2 * layer + 1, part(1 - core, width // 2), :]
    rows = pl.ds(c * CHUNK, CHUNK)
    summed[...] = pre[rows, :] + jnp.dot(mean_other[rows, :], right, preferred_element_type=jnp.float32)
    for begin in range(0, CHUNK, 128):
        x = summed[begin : begin + 128, :]
        mu = jnp.mean(x, axis=1, keepdims=True)
        centred = x - mu
        var = jnp.mean(centred * centred, axis=1, keepdims=True)
        value = jnp.maximum(centred * lax.rsqrt(var + 1e-05) * gain, 0.0)
        yield c * CHUNK + begin, value.astype(mean_other.dtype)


def dense_kernel(layer, blocks, pre, mean_other, gathered, h_out, outgoing, summed):
    core = lax.axis_index("dc")
    for c in range(pre.shape[0] // CHUNK):
        for begin, value in layer_rows(layer, core, c, pre, mean_other, gathered, summed.at[c]):
            h_out[begin : begin + 128, :] = value
    for j in range(outgoing.shape[0]):
        outgoing[j] = h_out[block_rows(blocks[reader_of(j)]), part(core, outgoing.shape[2])]


def dense(layer, blocks, pre, mean_other, gathered):
    rows, width = pre.shape
    return call(
        functools.partial(dense_kernel, layer),
        "dense",
        (SMEM,) + (VMEM,) * 3,
        [like(mean_other, pre.shape), like(mean_other, (blocks.shape[0], ROWS, width // 2))],
        (VMEM, VMEM),
        [pltpu.VMEM((rows // CHUNK, CHUNK, width), jnp.float32)],
    )(blocks, pre, mean_other, gathered)


def last_dense_kernel(pre, mean_other, gathered, *rest):
    *kept, leaving, summed, sems = rest
    core, last = lax.axis_index("dc"), N_LAYERS - 1
    half_rows = leaving.shape[1]
    copies = [
        pltpu.make_async_copy(source.at[part(core, half_rows)], leaving.at[ring_place(layer)], sems.at[layer])
        for layer, source in enumerate(kept)
    ]
    for copy in copies:
        copy.start()
    for c in range(half_rows // CHUNK):
        for begin, value in layer_rows(last, core, c, pre, mean_other, gathered, summed.at[c]):
            leaving[ring_place(last), begin : begin + 128, :] = value
    for copy in copies:
        copy.wait()


def last_dense(pre, mean_other, gathered, kept):
    half_rows, width = pre.shape
    (out,) = call(
        last_dense_kernel,
        "last_dense",
        (VMEM,) * 3 + (HBM,) * len(kept),
        [like(mean_other, (N_LAYERS, half_rows, width))],
        (VMEM,),
        [
            pltpu.VMEM((half_rows // CHUNK, CHUNK, width), jnp.float32),
            pltpu.SemaphoreType.DMA((N_LAYERS - 1,)),
        ],
    )(pre, mean_other, gathered, *kept)
    return out


def finish_kernel(crossing, source, *rest):
    out, sems = rest[-2:]
    core, chunk = lax.axis_index("dc"), source.shape[1]
    half = 1 - core if crossing else core
    pieces = []
    for g in range(2):
        piece = source.at[g] if crossing else source.at[2 * core + g]
        pieces.append((piece, out.at[g, part(half, chunk)]))
    run_copies(pieces, sems)


def finish(crossing, source, *results):
    _, chunk, width = source.shape
    (out,) = call(
        functools.partial(finish_kernel, crossing),
        "finish",
        (VMEM,) + (HBM,) * len(results),
        [like(source, (2, 2 * chunk, width))],
        (HBM,),
        [pltpu.SemaphoreType.DMA((2,))],
        input_output_aliases={1: 0} if crossing else {},
    )(source, *results)
    return out


def ring_place(section):
    return section % 2 * 2 + section // 2


def theirs_kernel(straight, out, sems):
    core = lax.axis_index("dc")
    run_copies([(straight.at[pl.ds(2 * (1 - core), 2)], out)], sems)


def theirs(straight):
    (out,) = call(
        theirs_kernel,
        "theirs",
        (VMEM,),
        [like(straight, (2,) + straight.shape[1:])],
        (VMEM,),
        [pltpu.SemaphoreType.DMA((2,))],
    )(straight)
    return out


def swap(value):
    return lax.ppermute(value, "dc", [(0, 1), (1, 0)])


def scalars(*values):
    return jnp.stack([jnp.asarray(v).astype(jnp.int32) for v in values])


def body(features, w_self, w_neigh, bias, gain, hubs, tile_src, counts):
    graph, parity = lax.axis_index("sm"), lax.axis_index("se")
    core = lax.axis_index("dc")
    section = 2 * graph + parity
    here = core == parity
    n_hubs = hubs.shape[1]
    place = scalars(graph, parity, core)

    outgoing, packed = front(hubs[:, :, 0], features, w_self, w_neigh, bias, gain)
    gathered = lax.all_gather(packed, SECTION + ("dc",))
    received = lax.all_to_all(outgoing, CORES, 0, 0, tiled=True)

    blocks = jnp.maximum(lax.dynamic_index_in_dim(hubs, graph, 0, keepdims=False).reshape(-1), 0)
    lists = jnp.concatenate(
        [blocks, lax.dynamic_index_in_dim(tile_src, graph, 0, keepdims=False).reshape(-1)]
    )
    lists = jnp.where(here, lists, swap(lists))
    blocks, tiles = lists[:n_hubs], lists[n_hubs:]
    counts, outgoing = lax.optimization_barrier((counts, outgoing))
    tile_counts, inverse = tally(place, counts)
    h, tile_counts, inverse = ready(
        place, features, tile_counts, inverse, swap(features), swap(tile_counts), swap(inverse)
    )
    kept = []
    for layer in range(N_LAYERS):
        if layer > 0:
            received = lax.all_to_all(outgoing, CHIPS, 0, 0, tiled=True)
        else:
            received, gathered = lax.optimization_barrier((received, gathered))
        last = layer == N_LAYERS - 1
        theirs_too, mean_mine = aggregate(last, tiles, h, received, tile_counts, inverse)
        mean_other = swap(theirs_too)
        pre = own_products(layer, h, mean_mine, gathered)
        if last:
            leaving = last_dense(pre, mean_other, gathered, kept)
        else:
            h, outgoing = dense(layer, blocks, pre, mean_other, gathered)
            kept.append(h)
    straight = lax.all_to_all(leaving, ("se", "sm"), 0, 0, tiled=True)
    crossed = swap(theirs(straight))
    results = finish(True, crossed, finish(False, straight))
    return results[None]


def solution(mesh):
    n_section, n_dp = mesh.shape["section"], mesh.shape["dp"]
    units = Mesh(mesh.devices.reshape(2, n_section // 2, n_dp // 2 // SIDE, SIDE, 2), SECTION + PARTS)
    placed = (
        P(None, PARTS, None),
        P(SECTION, None, None),
        P(SECTION, None, None),
        P(SECTION, None),
        P(SECTION, None),
        P(None, None, PARTS),
        P(None, PARTS, None),
        P(None, PARTS, None, None, None),
    )
    return jax.shard_map(
        body, mesh=units, in_specs=placed, out_specs=P(SECTION, None, PARTS, None), check_vma=False
    )
```
